128 devices in a mesh: segment: 8 (over z, x_lo), coil: 16 (over y, x_hi, core).
Axes of the slice: x: 4 (x_hi: 2, x_lo: 2; x = x_hi * 2 + x_lo), y: 4, z: 4, core: 2. Of those that a mesh axis runs over, the one named last changes fastest.
Arguments:
- measured: float32 [16, 2, 320, 128], P('coil'), may hold values from -6 to 6
- coil_maps: float32 [16, 2, 320, 128], P('coil'), may hold values from -4 to 4
- line_mask: int32 [16, 320], replicated, may hold values 0 or 1
- first_filters: float32 [8, 64, 18], P('segment'), may hold values from -1.5 to 1.5
- second_filters: float32 [8, 18, 64], P('segment'), may hold values from -0.075 to 0.075
- step_sizes: float32 [8], P('segment'), may hold values from 0.2 to 1
- final_cotangent: float32 [16, 2, 320, 128], P('coil'), may hold values from -6 to 6
Outputs:
- kspace_grads: float32 [8, 16, 2, 320, 128], P('segment', 'coil')
- first_grads: float32 [8, 64, 18], P('segment')
- second_grads: float32 [8, 18, 64], P('segment')
- step_grads: float32 [8], P('segment')
The draws below stay inside these ranges and needn't reach their ends.
All inputs are finite; a program needn't handle non-finite values.
Results may differ from the reference program's by a relative error of at most 0.0003.
Values sent between devices are 32-bit elements; how exact they have to be, the bound alone decides.
A program may use at most 320 MiB of HBM per device.

```python
import math
from functools import partial
import jax
import jax.numpy as jnp
from jax import lax

H = 320
W = 8
CH = 64
SLICES = 16
COILS = 16
CASC = 8


def place_ends(values, rng, smallest, top_value):
    extent = values.shape
    index_at = [jax.random.randint(jax.random.fold_in(rng, axis), (), 0, extent[axis]) for axis in range(len(extent))]
    values = values.at[tuple(index_at)].set(smallest)
    longest = extent.index(max(extent))
    index_at[longest] = (index_at[longest] + 1) % extent[longest]
    return values.at[tuple(index_at)].set(top_value)


def shard_levels(own_key, extent, shards, least, largest):
    def one(position, parts):
        steps = jax.random.uniform(jax.random.fold_in(jax.random.fold_in(own_key, 6), position), (parts,), jnp.float32, least / len(shards), largest / len(shards))
        return jnp.repeat(jnp.exp(steps), extent[position] // parts).reshape((-1,) + (1,) * (len(extent) - position - 1))

    gain = one(*shards[0])
    for cut in shards[1:]:
        gain = gain * one(*cut)
    return gain


def scatter_about(rng, shape, width, reach, shards=(), kind=jnp.bfloat16):
    entries = width * jax.random.normal(rng, shape, jnp.float32)
    if shards:
        entries = entries * shard_levels(rng, shape, shards, -0.22, 0.18)
    return jnp.clip(entries, -reach, reach).astype(kind)


def setup_inputs(seed: int = 0) -> dict:
    key_list = jax.random.split(jax.random.key(seed), 8)
    measured = scatter_about(key_list[0], (COILS, 2, H, SLICES * W), 1.0, 6.0, ((0, 16),), jnp.float32)
    coil_maps = scatter_about(key_list[1], (COILS, 2, H, SLICES * W), 0.3, 4.0, ((0, 16),), jnp.float32)
    line_mask = place_ends((jax.random.randint(key_list[2], (SLICES, H), 0, 3) < 1).astype(jnp.int32), jax.random.fold_in(key_list[2], 1), 0, 1)
    first_filters = scatter_about(key_list[3], (CASC, CH, 18), 18 ** -0.5, 1.5, ((0, 8),), jnp.float32)
    second_filters = scatter_about(key_list[4], (CASC, 18, CH), 0.0125, 0.075, ((0, 8),), jnp.float32)
    step_sizes = jnp.clip(jnp.exp(math.log(1.0) - 1.609438 * jax.random.uniform(key_list[5], (CASC,), jnp.float32) ** shard_levels(key_list[5], (CASC,), ((0, 8),), -0.2, 0.2)), 0.2, 1.0)
    final_cotangent = scatter_about(key_list[6], (COILS, 2, H, SLICES * W), 1.0, 6.0, ((0, 16),), jnp.float32)
    return dict(measured=measured, coil_maps=coil_maps, line_mask=line_mask, first_filters=first_filters, second_filters=second_filters, step_sizes=step_sizes, final_cotangent=final_cotangent)


PRECISE = lax.Precision.HIGHEST
tap_offsets = ((-1, -1), (-1, 0), (-1, 1), (0, -1), (0, 0), (0, 1), (1, -1), (1, 0), (1, 1))

def tables(line_count):
    positions = jnp.arange(line_count, dtype=jnp.int32)
    products = positions[:, None] * positions[None, :] % line_count
    angles = 2.0 * jnp.pi / line_count * products.astype(jnp.float32)
    factor = 1.0 / jnp.sqrt(jnp.float32(line_count))
    return (jnp.cos(angles) * factor, jnp.sin(angles) * factor)

def multiply_lines(table, operand):
    return jnp.einsum('uh,chx->cux', table, operand, precision=PRECISE)

def multiply_slices(table, operand, slice_width):
    count, lines, columns = operand.shape
    shaped = operand.reshape(count, lines, columns // slice_width, slice_width)
    result = jnp.einsum('us,chsw->chuw', table, shaped, precision=PRECISE)
    return result.reshape(count, lines, table.shape[0] * slice_width)

def rotate(cosine_table, sine_table, real_part, imag_part, applier, inverse):
    if inverse:
        out_real = applier(cosine_table, real_part) - applier(sine_table, imag_part)
        out_imag = applier(cosine_table, imag_part) + applier(sine_table, real_part)
    else:
        out_real = applier(cosine_table, real_part) + applier(sine_table, imag_part)
        out_imag = applier(cosine_table, imag_part) - applier(sine_table, real_part)
    return (out_real, out_imag)

def transform(kspace, line_tables, slice_tables, slice_width, inverse):
    real_part, imag_part = rotate(line_tables[0], line_tables[1], kspace[:, 0], kspace[:, 1], multiply_lines, inverse)
    real_part, imag_part = rotate(slice_tables[0], slice_tables[1], real_part, imag_part, partial(multiply_slices, slice_width=slice_width), inverse)
    return jnp.stack([real_part, imag_part], axis=1)

def conj_product(coil_maps, kspace):
    real_part = coil_maps[:, 0] * kspace[:, 0] + coil_maps[:, 1] * kspace[:, 1]
    imag_part = coil_maps[:, 0] * kspace[:, 1] - coil_maps[:, 1] * kspace[:, 0]
    return jnp.stack([lax.optimization_barrier(jnp.sum(real_part, axis=0)), lax.optimization_barrier(jnp.sum(imag_part, axis=0))])

def spread(coil_maps, picture):
    real_part = coil_maps[:, 0] * picture[0] - coil_maps[:, 1] * picture[1]
    imag_part = coil_maps[:, 0] * picture[1] + coil_maps[:, 1] * picture[0]
    return jnp.stack([real_part, imag_part], axis=1)

def moved(values, row_shift, col_shift, slice_width):
    total = values.shape[-1]
    margin = slice_width + 1
    padded = jnp.pad(values, ((0, 0), (margin, margin)))
    offset = margin + row_shift * slice_width + col_shift
    shifted = lax.slice_in_dim(padded, offset, offset + total, axis=1)
    column = jnp.arange(total, dtype=jnp.int32) % slice_width
    inside = (column + col_shift >= 0) & (column + col_shift < slice_width)
    return jnp.where(inside[None, :], shifted, jnp.zeros_like(shifted))

def network(picture, filters_in, filters_out, slice_width):
    stacked = jnp.stack([moved(picture, pair[0], pair[1], slice_width) for pair in tap_offsets])
    stacked = jnp.transpose(stacked, (1, 0, 2)).reshape(18, picture.shape[-1])
    hidden = jax.nn.silu(jnp.dot(filters_in, stacked, precision=PRECISE))
    response = jnp.dot(filters_out, hidden, precision=PRECISE).reshape(2, 9, picture.shape[-1])
    result = jnp.zeros_like(picture)
    for number, pair in enumerate(tap_offsets):
        result = result + moved(response[:, number], pair[0], pair[1], slice_width)
    return result

def refine(picture, filters_in, filters_out, slice_width):
    line_count = picture.shape[1]
    columns = picture.shape[2]
    count = columns // slice_width
    per_slice = picture.reshape(2, line_count, count, slice_width).transpose(2, 0, 1, 3)
    per_slice = per_slice.reshape(count, 2, line_count * slice_width)
    outcome = jax.vmap(lambda single: network(single, filters_in, filters_out, slice_width))(per_slice)
    outcome = outcome.reshape(count, 2, line_count, slice_width).transpose(1, 2, 0, 3)
    return outcome.reshape(2, line_count, columns)

def cascade(kspace, filters_in, filters_out, step_size, coil_maps, sampled_data, sampled, line_tables, slice_tables):
    combined = conj_product(coil_maps, transform(kspace, line_tables, slice_tables, W, True))
    refined = refine(combined, filters_in, filters_out, W)
    extra = transform(spread(coil_maps, refined), line_tables, slice_tables, W, False)
    return kspace - step_size * sampled * (kspace - sampled_data) + extra

def reference(measured, coil_maps, line_mask, first_filters, second_filters, step_sizes, final_cotangent):
    line_tables = tables(H)
    slice_tables = tables(SLICES)
    sampled = jnp.repeat(line_mask.T.astype(jnp.float32), W, axis=1)
    sampled_data = measured * sampled
    inputs = []
    current = sampled_data
    for number in range(CASC):
        inputs.append(current)
        current = cascade(current, first_filters[number], second_filters[number], step_sizes[number], coil_maps, sampled_data, sampled, line_tables, slice_tables)
    flowing = final_cotangent
    grads_k = [None] * CASC
    grads_in = [None] * CASC
    grads_out = [None] * CASC
    grads_step = [None] * CASC
    for number in reversed(range(CASC)):

        def single(kspace, filters_in, filters_out, step_size):
            return cascade(kspace, filters_in, filters_out, step_size, coil_maps, sampled_data, sampled, line_tables, slice_tables)
        _, pullback = jax.vjp(single, inputs[number], first_filters[number], second_filters[number], step_sizes[number])
        flowing, grad_in, grad_out, grad_step = pullback(flowing)
        grads_k[number] = flowing
        grads_in[number] = grad_in
        grads_out[number] = grad_out
        grads_step[number] = grad_step
    return (jnp.stack(grads_k), jnp.stack(grads_in), jnp.stack(grads_out), jnp.stack(grads_step))
```

```python
import functools

import jax
import jax.numpy as jnp
import ml_dtypes
import numpy as np
from jax import lax
from jax.experimental import pallas as pl
from jax.experimental.pallas import tpu as pltpu
from jax.sharding import PartitionSpec as P

F32 = jnp.float32
BF16 = jnp.bfloat16
LINES = 320
QUARTER = 80
LANES = 128
WIDTH = 8
SLICES = 16
COILS = 16
CASC = 8
STEPS = 2 * CASC
HIDDEN = 64
MESH = pl.DeviceIdType.MESH


def stacked(table):
    high = table.astype(ml_dtypes.bfloat16)
    low = (table - high.astype(np.float64)).astype(ml_dtypes.bfloat16)
    return np.concatenate([high, high, low], axis=-2)


@functools.lru_cache(maxsize=None)
def constants():
    forward = np.zeros((4, 256, 256))
    inverse = np.zeros((4, 256, 256))
    v = np.arange(QUARTER)[:, None]
    b = np.arange(QUARTER)[None, :]
    re, im = slice(0, QUARTER), slice(LANES, LANES + QUARTER)
    for m in range(4):
        angle = 2 * np.pi * (((4 * v + m) * b) % LINES) / LINES
        cosine = np.cos(angle) / np.sqrt(LINES)
        sine = np.sin(angle) / np.sqrt(LINES)
        forward[m, re, re] = cosine.T
        forward[m, re, im] = -sine.T
        forward[m, im, re] = sine.T
        forward[m, im, im] = cosine.T
        inverse[m, re, re] = cosine
        inverse[m, re, im] = sine
        inverse[m, im, re] = -sine
        inverse[m, im, im] = cosine
    tf = stacked(forward)
    ti = stacked(inverse)
    tft = np.ascontiguousarray(np.swapaxes(tf, 1, 2))

    perm = np.zeros((LANES, LANES), np.float32)
    dz = np.zeros((256, 256))
    for w in range(WIDTH):
        for s in range(SLICES):
            perm[w * SLICES + s, s * WIDTH + w] = 1
            for kz in range(SLICES):
                angle = 2 * np.pi * (s * kz % SLICES) / SLICES
                row, lane = w * SLICES + s, kz * WIDTH + w
                dz[row, lane] = np.cos(angle) / 4
                dz[row, LANES + lane] = -np.sin(angle) / 4
                dz[LANES + row, lane] = np.sin(angle) / 4
                dz[LANES + row, LANES + lane] = np.cos(angle) / 4
    dz = stacked(dz)

    rep = np.zeros((SLICES, LANES), np.float32)
    cz = np.zeros((WIDTH, 32, LANES), np.float32)
    gc = np.zeros((SLICES, 32, LANES), np.float32)
    for kz in range(SLICES):
        rep[kz, kz * WIDTH : (kz + 1) * WIDTH] = 1
        for s in range(SLICES):
            angle = 2 * np.pi * (s * kz % SLICES) / SLICES
            for w in range(WIDTH):
                cz[w, s, kz * WIDTH + w] = np.cos(angle) / 4
                cz[w, 16 + s, kz * WIDTH + w] = np.sin(angle) / 4
            for other in range(SLICES):
                angle = 2 * np.pi * ((s - other) * kz % SLICES) / SLICES
                gc[s, other, kz * WIDTH] = np.cos(angle) / 16
                gc[s, 16 + other, kz * WIDTH] = np.sin(angle) / 16

    expand = np.zeros((2, LANES, 4 * 256), np.float32)
    choose = np.zeros((2, 3 * 64, LANES), np.float32)
    fold = np.zeros((2, 24, LANES), np.float32)
    amask = np.zeros((64, 256), np.float32)
    gmask = np.zeros((256, LANES), np.float32)
    for ch in range(2):
        for dh in range(3):
            for dw in range(3):
                taps = (ch * 9 + dh * 3 + dw, ch * 9 + (2 - dh) * 3 + (2 - dw))
                for way in range(2):
                    for a in range(4):
                        lane = dw * 24 + dh * 8 + a * 2 + ch
                        expand[way, taps[way], a * 256 + lane] = 1
                        expand[way, taps[way], a * 256 + 72 + lane] = 1
                        expand[way, 24 + taps[way], a * 256 + 144 + lane] = 1
                        fold[way, taps[way], lane] = 1
                        for hl in range(2):
                            row = hl * 32 + dh * 8 + a * 2 + ch
                            choose[way, dw * 64 + row, hl * 24 + taps[way]] = 1
                            amask[row, a * 64 : (a + 1) * 64] = 1
                        gmask[a * 64 : (a + 1) * 64, lane] = 1
    bf = ml_dtypes.bfloat16
    return (
        tf, ti, tft, dz, perm, rep, cz, gc,
        expand.astype(bf), choose.astype(bf), fold, amask, gmask,
    )


def exact_nt(left, right):
    return lax.dot_general(
        left, right, (((1,), (1,)), ((), ())),
        precision=lax.Precision.HIGHEST, preferred_element_type=F32,
    )


def product(left, right):
    return jnp.dot(left, right, preferred_element_type=F32)


def product_nt(left, right):
    return lax.dot_general(left, right, (((1,), (1,)), ((), ())), preferred_element_type=F32)


def parts(values):
    high = values.astype(BF16)
    low = (values - high.astype(F32)).astype(BF16)
    return high, low


def triple(re, im):
    re_high, re_low = parts(re)
    im_high, im_low = parts(im)
    return jnp.concatenate([re_high, im_high, re_low, im_low, re_high, im_high], axis=1)


def shifted(tile):
    lane = lax.broadcasted_iota(jnp.int32, (8, LANES), 1)
    row = lax.broadcasted_iota(jnp.int32, (8, LANES), 0)
    zero = jnp.zeros_like(tile)
    last = QUARTER - 1
    next_first = pltpu.roll(pltpu.roll(tile, last, 1), 6, 0)
    after = jnp.where(
        lane < last,
        pltpu.roll(tile, LANES - 1, 1),
        jnp.where((lane == last) & (row < 6), next_first, zero),
    )
    previous_last = pltpu.roll(pltpu.roll(tile, LANES - last, 1), 2, 0)
    before = jnp.where(
        (lane >= 1) & (lane < QUARTER),
        pltpu.roll(tile, 1, 1),
        jnp.where((lane == 0) & (row >= 2), previous_last, zero),
    )
    return before, after


def quarters_to_residues(p):
    t0 = [p[0][k] + p[2][k] for k in range(2)]
    t1 = [p[0][k] - p[2][k] for k in range(2)]
    t2 = [p[1][k] + p[3][k] for k in range(2)]
    t3 = [p[1][k] - p[3][k] for k in range(2)]
    return (
        (t0[0] + t2[0], t0[1] + t2[1]),
        (t1[0] + t3[1], t1[1] - t3[0]),
        (t0[0] - t2[0], t0[1] - t2[1]),
        (t1[0] - t3[1], t1[1] + t3[0]),
    )


def residues_to_quarters(z):
    t0 = [z[0][k] + z[2][k] for k in range(2)]
    t1 = [z[0][k] - z[2][k] for k in range(2)]
    t2 = [z[1][k] + z[3][k] for k in range(2)]
    t3 = [z[1][k] - z[3][k] for k in range(2)]
    return (
        (t0[0] + t2[0], t0[1] + t2[1]),
        (t1[0] - t3[1], t1[1] + t3[0]),
        (t0[0] - t2[0], t0[1] - t2[1]),
        (t1[0] + t3[1], t1[1] - t3[0]),
    )


def inverse_lines(v, ti_ref):
    z = []
    for m in range(4):
        result = product(triple(*v[m]), ti_ref[m])
        z.append((result[:, :LANES], result[:, LANES:]))
    return residues_to_quarters(z)


def kernel(
    measured, maps, cotangent, mask, pack,
    tf, ti, tft, dz, perm, rep, cz, gc, expand, choose, fold, amask, gmask,
    grad_k, grad_w,
    sampled, masked, own_maps, maps_land, maps_all, lattice, partial_out, partial_land,
    weights, w_in, w_out, state, gathered, slope, centre, taps_saved, hidden, spectrum,
    energy, memory, final, sums, q_plain, q_masked, q_out, q_land, w_send, w_land, w_all,
    pack_send, pack_recv, part_send, part_recv, maps_send, maps_recv,
    near_send, near_recv, far_send, far_recv, q_send, q_recv, ws_send, ws_recv, wa_send, wa_recv,
):
    w = lax.axis_index("segment")
    s = lax.axis_index("coil")

    def send(source, target, send_sem, recv_sem, axis, place):
        pltpu.make_async_remote_copy(
            src_ref=source, dst_ref=target, send_sem=send_sem, recv_sem=recv_sem,
            device_id={axis: place}, device_id_type=MESH,
        ).start()

    def finish(extent, sem):
        pltpu.make_async_copy(extent, extent, sem).wait()

    segment_peers = [lax.rem(w + k, WIDTH) for k in range(1, WIDTH)]
    coil_peers = [lax.rem(s + k, COILS) for k in range(1, COILS)]

    barrier = pltpu.get_barrier_semaphore()
    for place in segment_peers:
        pl.semaphore_signal(barrier, inc=1, device_id={"segment": place}, device_id_type=MESH)
    for place in coil_peers:
        pl.semaphore_signal(barrier, inc=1, device_id={"coil": place}, device_id_type=MESH)
    pl.semaphore_wait(barrier, WIDTH - 1 + COILS - 1)

    weights[w] = pack[...]
    for place in segment_peers:
        send(weights.at[w], weights.at[w], pack_send, pack_recv, "segment", place)

    flags = mask[...].astype(F32)
    sampled[...] = lax.dot_general(
        flags, rep[...], (((0,), (0,)), ((), ())), preferred_element_type=F32
    )
    spots = sampled[...]
    for k in range(2):
        masked[0, k] = measured[k] * spots
        masked[1, k] = cotangent[k]
        masked[2, k] = cotangent[k] * spots

    own_maps[...] = jnp.zeros_like(own_maps)
    lattice[...] = jnp.zeros_like(lattice)
    for k in range(2):
        for a in range(4):
            own_maps[2 * a + k, :, :QUARTER] = exact_nt(
                perm[...], maps[k, a * QUARTER : (a + 1) * QUARTER, :]
            )
    here = pl.multiple_of(w * SLICES, SLICES)
    for k in range(8):
        maps_land[s, k] = own_maps[k, pl.ds(here, SLICES), :]

    hidden[...] = jnp.zeros_like(hidden)
    spectra = []
    for m in range(4):
        for field in range(3):
            rows_re = masked[field, 0, pl.ds(m, QUARTER, stride=4), :]
            rows_im = masked[field, 1, pl.ds(m, QUARTER, stride=4), :]
            from_re = exact_nt(cz[w], rows_re)
            from_im = exact_nt(cz[w], rows_im)
            place = pl.ds(field * SLICES, SLICES)
            hidden[place, :QUARTER] = from_re[:16] - from_im[16:]
            hidden[place, LANES : LANES + QUARTER] = from_im[:16] + from_re[16:]
        spectra.append((hidden[:48, :LANES], hidden[:48, LANES : 2 * LANES]))
    images = inverse_lines(spectra, ti)
    for a in range(4):
        map_re, map_im = maps_land[s, 2 * a], maps_land[s, 2 * a + 1]
        for field in range(3):
            re = images[a][0][field * 16 : (field + 1) * 16]
            im = images[a][1][field * 16 : (field + 1) * 16]
            row = field * 8 + 2 * a
            partial_out[pl.ds(row, SLICES, stride=32), :] = map_re * re + map_im * im
            partial_out[pl.ds(row + 1, SLICES, stride=32), :] = map_re * im - map_im * re
        power = map_re * map_re + map_im * map_im
        partial_out[pl.ds(24 + 2 * a, SLICES, stride=32), :] = power
        partial_out[pl.ds(25 + 2 * a, SLICES, stride=32), :] = power

    for place in coil_peers:
        send(
            partial_out.at[pl.ds(pl.multiple_of(place * 32, 32), 32)],
            partial_land.at[s], part_send, part_recv, "coil", place,
        )
    for place in coil_peers:
        send(maps_land.at[s], maps_land.at[s], maps_send, maps_recv, "coil", place)
    partial_land[s] = partial_out[pl.ds(pl.multiple_of(s * 32, 32), 32), :]

    def prepare(step):
        way = (step >= CASC).astype(jnp.int32)
        cascade = jnp.where(step < CASC, step, STEPS - 1 - step)
        raw = weights[cascade]
        lane = lax.broadcasted_iota(jnp.int32, raw.shape, 1)
        turned = pltpu.roll(raw, 64, 1)
        first = jnp.where(lane < 64, raw, turned)
        second = jnp.where(lane < 64, turned, raw)
        enter = jnp.where(way == 0, first, second)
        leave = jnp.where(way == 0, second, first)

        def columns(values):
            high = values.astype(BF16).astype(F32)
            return jnp.concatenate([high, values - high, jnp.zeros((80, LANES), F32)], axis=0)

        flat = columns(enter).T[:64].astype(BF16)
        wide = product(flat, expand[way]).astype(BF16)
        for a in range(4):
            w_in[a * 64 : (a + 1) * 64, :] = wide[:, a * 256 : (a + 1) * 256]
        tall = product(choose[way], columns(leave).astype(BF16))
        for j in range(3):
            block = tall[j * 64 : (j + 1) * 64]
            block = jnp.concatenate([block, block], axis=1) * amask[...]
            w_out[:, j * 256 : (j + 1) * 256] = block.astype(BF16)

    finish(weights.at[pl.ds(0, WIDTH - 1)], pack_recv)
    prepare(jnp.int32(0))

    def near(step):
        for distance in (1, -1, 2, -2):
            place = lax.rem(w + distance + WIDTH, WIDTH)
            send(
                state.at[step, 2], state.at[step, 2 - distance],
                near_send.at[step], near_recv.at[step], "segment", place,
            )

    finish(partial_land.at[pl.ds(0, COILS - 1)], part_recv)
    total = partial_land[0]
    for k in range(1, COILS):
        total = total + partial_land[k]
    state[0, 2] = total[0:8]
    near(0)
    state[CASC, 2] = total[8:16]
    near(CASC)
    energy[...] = total[24:32]
    final[...] = total[16:24]

    for m in range(4):
        kernel_rows = exact_nt(gc[s], sampled[pl.ds(m, QUARTER, stride=4), :])
        lattice[m, 0, :, :QUARTER] = kernel_rows[:16]
        lattice[m, 1, :, :QUARTER] = kernel_rows[16:]

    memory[...] = jnp.zeros_like(memory)
    sums[...] = jnp.zeros_like(sums)
    q_plain[...] = jnp.zeros_like(q_plain)
    q_masked[...] = jnp.zeros_like(q_masked)

    def normal(step):
        for block in range(4):
            p = []
            for a in range(4):
                res, ims = [], []
                for inner in range(4):
                    other = block * 4 + inner
                    re = gathered[step, other, 2 * a : 2 * a + 1, :]
                    im = gathered[step, other, 2 * a + 1 : 2 * a + 2, :]
                    map_re = maps_all[2 * a, pl.ds(other * 16, 16), :]
                    map_im = maps_all[2 * a + 1, pl.ds(other * 16, 16), :]
                    res.append(map_re * re - map_im * im)
                    ims.append(map_re * im + map_im * re)
                p.append((jnp.concatenate(res, axis=0), jnp.concatenate(ims, axis=0)))
            z = quarters_to_residues(p)
            for m in range(4):
                spectrum[m, pl.ds(block * 64, 64), :] = triple(*z[m])
        v = []
        for m in range(4):
            x = product(spectrum[m], tf[m])
            re = jnp.zeros((16, LANES), F32)
            im = jnp.zeros((16, LANES), F32)
            for other in range(SLICES):
                g_re = lattice[m, 0, other : other + 1, :]
                g_im = lattice[m, 1, other : other + 1, :]
                x_re = x[other * 16 : (other + 1) * 16, :LANES]
                x_im = x[other * 16 : (other + 1) * 16, LANES:]
                re = re + (g_re * x_re - g_im * x_im)
                im = im + (g_re * x_im + g_im * x_re)
            v.append((re, im))
        y = inverse_lines(v, ti)
        rows = []
        mine = pl.ds(pl.multiple_of(s * 16, 16), 16)
        for a in range(4):
            map_re, map_im = maps_all[2 * a, mine, :], maps_all[2 * a + 1, mine, :]
            rows.append(jnp.sum(map_re * y[a][0] + map_im * y[a][1], axis=0, keepdims=True))
            rows.append(jnp.sum(map_re * y[a][1] - map_im * y[a][0], axis=0, keepdims=True))
        return jnp.concatenate(rows, axis=0)

    def cascade_of(step):
        return jnp.where(step < CASC, step, STEPS - 1 - step)

    def step_size(cascade):
        return weights[cascade, 18:19, :]

    def collect(cascade):
        keep = 1.0 - step_size(cascade)
        slot = STEPS - 1 - cascade
        images = gathered[slot].reshape(SLICES * 8, LANES)
        q_plain[...] = q_plain[...] + images
        q_masked[...] = q_masked[...] * keep + images
        q_out[cascade, 0] = q_plain[...]
        q_out[cascade, 1] = q_masked[...]

        @pl.when(w == cascade)
        def _():
            q_land[w] = q_out[cascade]

        @pl.when(w != cascade)
        def _():
            send(
                q_out.at[cascade], q_land.at[w], q_send.at[cascade], q_recv, "segment", cascade
            )

    def turn(step, carry):
        backward = step >= CASC
        cascade = cascade_of(step)
        finish(state.at[step, pl.ds(0, 4)], near_recv.at[step])

        taps = []
        for column in range(5):
            place = w + (column - 2)
            tile = state[step, column]
            tile = jnp.where((place >= 0) & (place < WIDTH), tile, jnp.zeros_like(tile))
            before, after = shifted(tile)
            taps += [before, tile, after]
        taps = jnp.concatenate(taps, axis=0)
        high = taps.astype(BF16).astype(F32)
        low = taps - high
        rest = jnp.zeros((40, LANES), F32)
        columns = []
        for j in range(3):
            span = slice(24 * j, 24 * j + 72)
            columns.append(jnp.concatenate([high[span], low[span], high[span], rest], axis=0))
        operand = jnp.concatenate(columns, axis=1).astype(BF16)
        lane = lax.broadcasted_iota(jnp.int32, (256, 3 * LANES), 1)
        place = w + lane // LANES - 1
        inside = (place >= 0) & (place < WIDTH)

        @pl.when(jnp.logical_not(backward))
        def _():
            before = product(w_in[...], operand)
            gate = 1.0 / (1.0 + jnp.exp(-before))
            after = before * gate
            zero = jnp.zeros_like(before)
            hidden[...] = jnp.where(inside, after, zero)
            slope[cascade] = jnp.where(inside, gate + after * (1.0 - gate), zero)
            centre[cascade] = after[:, LANES : 2 * LANES]
            taps_saved[cascade] = taps[24:96]

        @pl.when(backward)
        def _():
            hidden[...] = product(w_in[...], operand) * slope[cascade]

        @pl.when(step != CASC - 1)
        def _():
            stack = jnp.concatenate([hidden[:, j * LANES : (j + 1) * LANES] for j in range(3)], axis=0)
            stack_high, stack_low = parts(stack)
            first = product(w_out[...], stack_high)
            second = product(w_out[0:32, :], stack_low)
            response = first[0:24] + first[32:56] + second[0:24]
            before, _ = shifted(response[0:8])
            _, after = shifted(response[16:24])
            gathered[step, s] = before + response[8:16] + after

        @pl.when((step < CASC - 2) | backward)
        def _():
            for place in coil_peers:
                send(
                    gathered.at[step, s], gathered.at[step, s],
                    far_send.at[step], far_recv.at[step], "coil", place,
                )

        @pl.when(step == 1)
        def _():
            finish(maps_land.at[pl.ds(0, COILS - 1)], maps_recv)
            for coil in range(COILS):
                for k in range(8):
                    maps_all[k, pl.ds(coil, SLICES, stride=16), :] = maps_land[coil, k]

        older = step - 1
        once = (step >= 1) & (step < CASC - 1)
        again = (step >= CASC + 1) & (step < STEPS - 1)

        @pl.when(once | again)
        def _():
            finish(gathered.at[older, pl.ds(0, COILS - 1)], far_recv.at[older])
            memory[...] = memory[...] * (1.0 - step_size(cascade_of(older))) + normal(older)

        @pl.when((step != CASC - 1) & (step != STEPS - 1))
        def _():
            answer = gathered[step, s]
            state[step + 1, 2] = (
                state[step, 2] - step_size(cascade) * memory[...] + energy[...] * answer
            )
            near(step + 1)

        @pl.when(step < CASC - 1)
        def _():
            sums[step + 1] = sums[step] * (1.0 - step_size(cascade)) + gathered[step, s]
            prepare(step + 1)

        @pl.when(step == CASC - 1)
        def _():
            memory[...] = final[...]
            prepare(step + 1)

        @pl.when(backward)
        def _():
            @pl.when(step < STEPS - 1)
            def _():
                prepare(step + 1)

            pad = jnp.zeros((56, LANES), F32)
            grads = []
            pairs = (
                (hidden[:, LANES : 2 * LANES], taps_saved[cascade]),
                (centre[cascade], taps[24:96]),
            )
            for values, around in pairs:
                left_high, left_low = parts(values)
                right_high, right_low = parts(jnp.concatenate([around, pad], axis=0))
                full = product_nt(
                    jnp.concatenate([left_high, left_low, left_high], axis=1),
                    jnp.concatenate([right_high, right_high, right_low], axis=1),
                ) * gmask[...]
                grads.append(full[0:64] + full[64:128] + full[128:192] + full[192:256])
            grads = jnp.concatenate(grads, axis=0)
            first = exact_nt(fold[0], grads)
            second = exact_nt(fold[1], grads)
            lanes = lax.broadcasted_iota(jnp.int32, (24, LANES), 1)
            rows = lax.broadcasted_iota(jnp.int32, (24, LANES), 0)
            sizes = -jnp.sum(sums[cascade] * memory[...], axis=0, keepdims=True)
            w_send[cascade] = jnp.where(
                rows == 18, sizes, jnp.where(lanes < 64, first, second)
            )

            @pl.when(w == cascade)
            def _():
                w_land[w] = w_send[cascade]

            @pl.when(w != cascade)
            def _():
                send(
                    w_send.at[cascade], w_land.at[w], ws_send.at[cascade], ws_recv,
                    "segment", cascade,
                )

            @pl.when(step == STEPS - 1)
            def _():
                finish(gathered.at[older, pl.ds(0, COILS - 1)], far_recv.at[older])

            @pl.when(step > CASC)
            def _():
                collect(cascade + 1)

        return carry

    lax.fori_loop(0, STEPS, turn, jnp.int32(0))

    finish(gathered.at[STEPS - 1, pl.ds(0, COILS - 1)], far_recv.at[STEPS - 1])
    collect(jnp.int32(0))

    finish(w_land.at[pl.ds(0, WIDTH - 1)], ws_recv)
    total = w_land[0]
    for k in range(1, WIDTH):
        total = total + w_land[k]
    w_all[s] = total
    for place in coil_peers:
        send(w_all.at[s], w_all.at[s], wa_send, wa_recv, "coil", place)

    keep = jnp.ones((1, LANES), F32)
    for cascade in range(CASC):
        factor = 1.0 - step_size(cascade)
        keep = jnp.where(cascade >= w, keep * factor, keep)

    finish(q_land.at[pl.ds(0, WIDTH - 1)], q_recv)
    p = []
    for a in range(4):
        map_re, map_im = own_maps[2 * a], own_maps[2 * a + 1]
        res, ims = [], []
        for image in range(2):
            q = [
                jnp.concatenate(
                    [q_land[k, image, pl.ds(2 * a + part, SLICES, stride=8), :] for k in range(WIDTH)],
                    axis=0,
                )
                for part in range(2)
            ]
            res.append(map_re * q[0] - map_im * q[1])
            ims.append(map_re * q[1] + map_im * q[0])
        p.append((jnp.concatenate(res, axis=0), jnp.concatenate(ims, axis=0)))
    z = quarters_to_residues(p)
    for m in range(4):
        lines = product_nt(tft[m], triple(*z[m]))
        outs = []
        for image in range(2):
            span = slice(image * LANES, (image + 1) * LANES)
            field = product(
                triple(lines[0:QUARTER, span], lines[LANES : LANES + QUARTER, span]), dz[...]
            )
            outs.append((field[:, :LANES], field[:, LANES:]))
        rows = pl.ds(m, QUARTER, stride=4)
        spots = sampled[rows, :]
        for k in range(2):
            seed = cotangent[k, rows, :]
            grad_k[k, rows, :] = jnp.where(spots > 0.5, keep * seed + outs[1][k], seed + outs[0][k])

    finish(w_all.at[pl.ds(0, COILS - 1)], wa_recv)
    total = w_all[0]
    for k in range(1, COILS):
        total = total + w_all[k]
    grad_w[...] = total

    finish(weights.at[pl.ds(0, WIDTH - 1)], pack_send)
    finish(partial_land.at[pl.ds(0, COILS - 1)], part_send)
    finish(maps_land.at[pl.ds(0, COILS - 1)], maps_send)
    finish(w_all.at[pl.ds(0, COILS - 1)], wa_send)

    def drain(step, carry):
        @pl.when((step < CASC - 2) | (step >= CASC))
        def _():
            finish(gathered.at[step, pl.ds(0, COILS - 1)], far_send.at[step])

        finish(state.at[step, pl.ds(0, 4)], near_send.at[step])

        @pl.when((step < CASC) & (step != w))
        def _():
            finish(q_out.at[step % CASC], q_send.at[step % CASC])
            finish(w_send.at[step % CASC], ws_send.at[step % CASC])

        return carry

    lax.fori_loop(0, STEPS, drain, jnp.int32(0))


def shards(measured, maps, mask, first_filters, second_filters, step_sizes, cotangent):
    body = jnp.concatenate([first_filters[0].T, second_filters[0]], axis=1)
    steps = jnp.broadcast_to(step_sizes[0], (6, LANES))
    pack = jnp.concatenate([body, steps], axis=0)
    tables = [jnp.asarray(table) for table in constants()]
    dma = pltpu.SemaphoreType.DMA
    scratch = [
        pltpu.VMEM((LINES, LANES), F32),
        pltpu.VMEM((3, 2, LINES, LANES), F32),
        pltpu.VMEM((8, LANES, LANES), F32),
        pltpu.VMEM((COILS, 8, SLICES, LANES), F32),
        pltpu.VMEM((8, SLICES * COILS, LANES), F32),
        pltpu.VMEM((4, 2, SLICES, LANES), F32),
        pltpu.VMEM((SLICES * 32, LANES), F32),
        pltpu.VMEM((COILS, 32, LANES), F32),
        pltpu.VMEM((CASC, 24, LANES), F32),
        pltpu.VMEM((256, 256), BF16),
        pltpu.VMEM((64, 768), BF16),
        pltpu.VMEM((STEPS, 5, 8, LANES), F32),
        pltpu.VMEM((STEPS, SLICES, 8, LANES), F32),
        pltpu.VMEM((CASC, 256, 3 * LANES), F32),
        pltpu.VMEM((CASC, 256, LANES), F32),
        pltpu.VMEM((CASC, 72, LANES), F32),
        pltpu.VMEM((256, 3 * LANES), F32),
        pltpu.VMEM((4, 256, 768), BF16),
        pltpu.VMEM((8, LANES), F32),
        pltpu.VMEM((8, LANES), F32),
        pltpu.VMEM((8, LANES), F32),
        pltpu.VMEM((CASC, 8, LANES), F32),
        pltpu.VMEM((SLICES * 8, LANES), F32),
        pltpu.VMEM((SLICES * 8, LANES), F32),
        pltpu.VMEM((CASC, 2, SLICES * 8, LANES), F32),
        pltpu.VMEM((WIDTH, 2, SLICES * 8, LANES), F32),
        pltpu.VMEM((CASC, 24, LANES), F32),
        pltpu.VMEM((WIDTH, 24, LANES), F32),
        pltpu.VMEM((COILS, 24, LANES), F32),
        dma, dma, dma, dma, dma, dma,
        dma((STEPS,)), dma((STEPS,)), dma((STEPS,)), dma((STEPS,)),
        dma((CASC,)), dma, dma((CASC,)), dma, dma, dma,
    ]
    whole = pl.BlockSpec(memory_space=pltpu.VMEM)
    operands = [measured[0], maps[0], cotangent[0], mask, pack] + tables
    grad_k, grad_w = pl.pallas_call(
        kernel,
        out_shape=[
            jax.ShapeDtypeStruct((2, LINES, LANES), F32),
            jax.ShapeDtypeStruct((24, LANES), F32),
        ],
        in_specs=[whole] * len(operands),
        out_specs=[whole, whole],
        scratch_shapes=scratch,
        compiler_params=pltpu.CompilerParams(
            collective_id=0, has_side_effects=True, vmem_limit_bytes=48 * 1024 * 1024
        ),
        name="cascades",
    )(*operands)
    first = grad_w[:18, :64].T
    second = grad_w[:18, 64:]
    return grad_k[None, None], first[None], second[None], jnp.sum(grad_w[18]).reshape(1)


def solution(mesh):
    in_specs = (
        P("coil", None, None, None),
        P("coil", None, None, None),
        P(),
        P("segment", None, None),
        P("segment", None, None),
        P("segment"),
        P("coil", None, None, None),
    )
    out_specs = (
        P("segment", "coil", None, None, None),
        P("segment", None, None),
        P("segment", None, None),
        P("segment"),
    )
    return jax.shard_map(shards, mesh=mesh, in_specs=in_specs, out_specs=out_specs, check_vma=False)
```

```python
import functools

import jax
import jax.numpy as jnp
import ml_dtypes
import numpy as np
from jax import lax
from jax.experimental import pallas as pl
from jax.experimental.pallas import tpu as pltpu
from jax.sharding import PartitionSpec as P

F32 = jnp.float32
BF16 = jnp.bfloat16
LINES = 320
QUARTER = 80
LANES = 128
WIDTH = 8
SLICES = 16
COILS = 16
CASC = 8
STEPS = 2 * CASC
HIDDEN = 64
MESH = pl.DeviceIdType.MESH
AROUND = sorted(
    [(dy, dx) for dy in range(4) for dx in range(4) if dy or dx],
    key=lambda d: -(min(d[0], 4 - d[0]) + min(d[1], 4 - d[1])),
)
LONG = 11
ROWS = (0, 1, 3, 2)


def stacked(table):
    high = table.astype(ml_dtypes.bfloat16)
    low = (table - high.astype(np.float64)).astype(ml_dtypes.bfloat16)
    return np.concatenate([high, high, low], axis=-2)


@functools.lru_cache(maxsize=None)
def constants():
    forward = np.zeros((4, 256, 256))
    inverse = np.zeros((4, 256, 256))
    v = np.arange(QUARTER)[:, None]
    b = np.arange(QUARTER)[None, :]
    re, im = slice(0, QUARTER), slice(LANES, LANES + QUARTER)
    for m in range(4):
        angle = 2 * np.pi * (((4 * v + m) * b) % LINES) / LINES
        cosine = np.cos(angle) / np.sqrt(LINES)
        sine = np.sin(angle) / np.sqrt(LINES)
        forward[m, re, re] = cosine.T
        forward[m, re, im] = -sine.T
        forward[m, im, re] = sine.T
        forward[m, im, im] = cosine.T
        inverse[m, re, re] = cosine
        inverse[m, re, im] = sine
        inverse[m, im, re] = -sine
        inverse[m, im, im] = cosine
    tf = stacked(forward)
    ti = stacked(inverse)
    tft = np.ascontiguousarray(np.swapaxes(tf, 1, 2))

    dz = np.zeros((256, 256))
    for w in range(WIDTH):
        for s in range(SLICES):
            for kz in range(SLICES):
                angle = 2 * np.pi * (s * kz % SLICES) / SLICES
                row, lane = w * SLICES + s, kz * WIDTH + w
                dz[row, lane] = np.cos(angle) / 4
                dz[row, LANES + lane] = -np.sin(angle) / 4
                dz[LANES + row, lane] = np.sin(angle) / 4
                dz[LANES + row, LANES + lane] = np.cos(angle) / 4
    dz = stacked(dz)

    rep = np.zeros((SLICES, LANES), np.float32)
    for kz in range(SLICES):
        rep[kz, kz * WIDTH : (kz + 1) * WIDTH] = 1
    outward = np.zeros((16, 48, LANES), np.float32)
    for g in range(WIDTH):
        for x_hi in range(2):
            for q in range(16):
                j = q % 8
                s = 2 * j + (g % 2 if j % 2 == x_hi else 1 - g % 2)
                w = 2 * (g // 2) + q // 8
                outward[2 * g + x_hi, 32 + q, s * WIDTH + w] = 1
                for kz in range(SLICES):
                    angle = 2 * np.pi * (s * kz % SLICES) / SLICES
                    outward[2 * g + x_hi, q, kz * WIDTH + w] = np.cos(angle) / 4
                    outward[2 * g + x_hi, 16 + q, kz * WIDTH + w] = np.sin(angle) / 4
    gc = np.zeros((SLICES, 32, LANES), np.float32)
    for kz in range(SLICES):
        for s in range(SLICES):
            for n in range(SLICES):
                other = 4 * ((s // 4 + ROWS[n // 4]) % 4) + n % 4
                angle = 2 * np.pi * ((s - other) * kz % SLICES) / SLICES
                gc[s, n, kz * WIDTH] = np.cos(angle) / 16
                gc[s, 16 + n, kz * WIDTH] = np.sin(angle) / 16

    expand = np.zeros((2, LANES, 4 * 256), np.float32)
    choose = np.zeros((2, 3 * 64, LANES), np.float32)
    fold = np.zeros((2, 24, LANES), np.float32)
    amask = np.zeros((64, 256), np.float32)
    gmask = np.zeros((256, LANES), np.float32)
    for ch in range(2):
        for dh in range(3):
            for dw in range(3):
                taps = (ch * 9 + dh * 3 + dw, ch * 9 + (2 - dh) * 3 + (2 - dw))
                for way in range(2):
                    for a in range(4):
                        lane = dw * 24 + dh * 8 + a * 2 + ch
                        expand[way, taps[way], a * 256 + lane] = 1
                        expand[way, taps[way], a * 256 + 72 + lane] = 1
                        expand[way, 24 + taps[way], a * 256 + 144 + lane] = 1
                        fold[way, taps[way], lane] = 1
                        for hl in range(2):
                            row = hl * 32 + dh * 8 + a * 2 + ch
                            choose[way, dw * 64 + row, hl * 24 + taps[way]] = 1
                            amask[row, a * 64 : (a + 1) * 64] = 1
                        gmask[a * 64 : (a + 1) * 64, lane] = 1
    bf = ml_dtypes.bfloat16
    wide = np.concatenate([tf.reshape(-1, 256), ti.reshape(-1, 256), dz], axis=0)
    misc = np.concatenate(
        [rep, fold.reshape(48, LANES), gmask, amask[:, :LANES], amask[:, LANES:]], axis=0
    )
    return wide, tft, expand.astype(bf), choose.astype(bf), misc, outward, gc


def product(left, right):
    return jnp.dot(left, right, preferred_element_type=F32)


def product_nt(left, right):
    return lax.dot_general(left, right, (((1,), (1,)), ((), ())), preferred_element_type=F32)


def parts(values):
    high = values.astype(BF16)
    low = (values - high.astype(F32)).astype(BF16)
    return high, low


def three(values):
    first = values.astype(BF16)
    rest = values - first.astype(F32)
    second = rest.astype(BF16)
    third = (rest - second.astype(F32)).astype(BF16)
    return jnp.concatenate([first, second, third], axis=1)


def triple(re, im):
    re_high, re_low = parts(re)
    im_high, im_low = parts(im)
    return jnp.concatenate([re_high, im_high, re_low, im_low, re_high, im_high], axis=1)


def shifted(tile):
    lane = lax.broadcasted_iota(jnp.int32, (8, LANES), 1)
    row = lax.broadcasted_iota(jnp.int32, (8, LANES), 0)
    zero = jnp.zeros_like(tile)
    last = QUARTER - 1
    next_first = pltpu.roll(pltpu.roll(tile, last, 1), 6, 0)
    after = jnp.where(
        lane < last,
        pltpu.roll(tile, LANES - 1, 1),
        jnp.where((lane == last) & (row < 6), next_first, zero),
    )
    previous_last = pltpu.roll(pltpu.roll(tile, LANES - last, 1), 2, 0)
    before = jnp.where(
        (lane >= 1) & (lane < QUARTER),
        pltpu.roll(tile, 1, 1),
        jnp.where((lane == 0) & (row >= 2), previous_last, zero),
    )
    return before, after


def quarters_to_residues(p):
    t0 = [p[0][k] + p[2][k] for k in range(2)]
    t1 = [p[0][k] - p[2][k] for k in range(2)]
    t2 = [p[1][k] + p[3][k] for k in range(2)]
    t3 = [p[1][k] - p[3][k] for k in range(2)]
    return (
        (t0[0] + t2[0], t0[1] + t2[1]),
        (t1[0] + t3[1], t1[1] - t3[0]),
        (t0[0] - t2[0], t0[1] - t2[1]),
        (t1[0] - t3[1], t1[1] + t3[0]),
    )


def residues_to_quarters(z):
    t0 = [z[0][k] + z[2][k] for k in range(2)]
    t1 = [z[0][k] - z[2][k] for k in range(2)]
    t2 = [z[1][k] + z[3][k] for k in range(2)]
    t3 = [z[1][k] - z[3][k] for k in range(2)]
    return (
        (t0[0] + t2[0], t0[1] + t2[1]),
        (t1[0] - t3[1], t1[1] + t3[0]),
        (t0[0] - t2[0], t0[1] - t2[1]),
        (t1[0] + t3[1], t1[1] - t3[0]),
    )


def inverse_lines(v, table):
    z = []
    for m in range(4):
        result = product(triple(*v[m]), table(m))
        z.append((result[:, :LANES], result[:, LANES:]))
    return residues_to_quarters(z)


def kernel(
    measured_hbm, maps_hbm, cotangent_hbm, mask_hbm, first_hbm, second_hbm, size_ref,
    wide_hbm, tft_hbm, expand_hbm, choose_hbm, misc_hbm, outward_hbm, gc_hbm,
    grad_k, grad_w,
    measured, maps, cotangent, mask, first_in, second_in,
    wide, tft, expand, choose, misc, outward, gc, load_sem,
    sampled, masked, turned_maps, maps_out, maps_land, maps_all, lattice, picked, partial_out, partial_land,
    ending_out, ending_land,
    weights, w_in, w_out, state, gathered, slope, centre, taps_saved, hidden, spectrum,
    energy, memory, final, sums, q_plain, q_masked, q_out, q_land, q_open, tail_land, late_land,
    w_send, w_land, w_pair, w_all,
    pack_send, pack_recv, part_send, part_recv, end_send, end_recv, maps_send, maps_recv,
    near_send, near_recv, far_send, far_recv, far_late, q_send, q_recv,
    tail_send, tail_recv, late_send, late_recv, pass_send, pass_recv,
    ws_send, ws_recv, wp_send, wp_recv, wa_send, wa_recv,
):
    g = lax.axis_index("segment")
    k = lax.axis_index("coil")
    z, x_lo = lax.div(g, 2), lax.rem(g, 2)
    pair, core = lax.div(k, 2), lax.rem(k, 2)
    y, x_hi = lax.div(pair, 2), lax.rem(pair, 2)
    w = 2 * z + core
    s = 2 * pair + x_lo
    x = 2 * x_hi + x_lo

    def role(at_w, at_s):
        return {
            "segment": 2 * lax.div(at_w, 2) + lax.rem(at_s, 2),
            "coil": 2 * lax.div(at_s, 2) + lax.rem(at_w, 2),
        }

    def around(displacement):
        dy, dx = displacement
        return role(w, 4 * lax.rem(y + dy, 4) + lax.rem(x + dx, 4))

    def place(at_g, at_k):
        return {"segment": at_g, "coil": at_k}

    receivers = []
    for dy in (2, 1, 3, 0):
        for flip in range(2):
            for at_core in range(2):
                if dy or flip:
                    at_k = 4 * lax.rem(y + dy, 4) + 2 * lax.rem(x_hi + flip, 2) + at_core
                    at_g = g if flip == 0 else 2 * z + 1 - x_lo
                    receivers.append((at_g, at_k, at_core))
    receivers.append((g, 2 * pair + 1 - core, 1 - core))
    segment_peers = [lax.rem(g + n, WIDTH) for n in range(1, WIDTH)]

    def send(source, target, send_sem, recv_sem, device):
        pltpu.make_async_remote_copy(
            src_ref=source, dst_ref=target, send_sem=send_sem, recv_sem=recv_sem,
            device_id=device, device_id_type=MESH,
        ).start()

    def finish(extent, sem):
        pltpu.make_async_copy(extent, extent, sem).wait()

    loads = (
        (maps_hbm, maps), (measured_hbm, measured), (mask_hbm, mask), (misc_hbm, misc),
        (outward_hbm.at[2 * g + x_hi], outward), (wide_hbm, wide),
        (first_hbm, first_in), (second_hbm, second_in), (cotangent_hbm, cotangent),
        (gc_hbm.at[s], gc), (expand_hbm, expand), (choose_hbm, choose), (tft_hbm, tft),
    )
    loads = [
        pltpu.make_async_copy(source, target, load_sem.at[n])
        for n, (source, target) in enumerate(loads)
    ]
    for load in loads[:6]:
        load.start()

    barrier = pltpu.get_barrier_semaphore()

    def greet(device):
        pl.semaphore_signal(barrier, inc=1, device_id=device, device_id_type=MESH)

    for dy, dx in AROUND:
        if dx:
            other = lax.rem(x + dx, 4)

            @pl.when(other != 3 - x)
            def _():
                greet(role(w, 4 * lax.rem(y + dy, 4) + other))

    for turn in (2, 1, 3):
        at_z = lax.rem(z + turn, 4)
        greet(place(2 * at_z + 1 - x_lo, k))
        for at_core in range(2):
            greet(place(2 * at_z + x_lo, 2 * pair + at_core))
    for at_g, at_k, _ in receivers:
        greet(place(at_g, at_k))
    for load in loads[6:]:
        load.start()

    def tf(m):
        return wide[m * 768 : (m + 1) * 768, :]

    def ti(m):
        return wide[3072 + m * 768 : 3072 + (m + 1) * 768, :]

    def dz():
        return wide[6144:6912, :]

    blank = jnp.zeros((LANES - QUARTER, LANES), F32)

    def padded(values):
        return jnp.concatenate([values, blank], axis=0)

    loads[0].wait()
    for part in range(2):
        for a in range(4):
            block = padded(maps[part, a * QUARTER : (a + 1) * QUARTER, :])
            turned_maps[2 * a + part] = block.T
    for at_core in range(2):
        lines = [
            turned_maps[plane, pl.ds(2 * z + at_core, SLICES, stride=WIDTH), :]
            for plane in range(8)
        ]
        maps_out[at_core] = jnp.concatenate(lines, axis=0).T[:QUARTER]
    maps_land[k] = maps_out[core]

    for load in loads[1:5]:
        load.wait()
    sampled[...] = lax.dot_general(
        mask[...].astype(F32), misc[0:16], (((0,), (0,)), ((), ())), preferred_element_type=F32
    )
    spots = sampled[...]
    for part in range(2):
        masked[0, part] = measured[part] * spots
    c_high, c_low = parts(outward[0:32, :])
    c_left = jnp.concatenate([c_high, c_high, c_low], axis=1)

    def to_images(fields):
        spectra = []
        for m in range(4):
            rows = pl.ds(m, QUARTER, stride=4)
            blocks = [padded(masked[field, part, rows, :]) for field in fields for part in range(2)]
            high, low = parts(jnp.concatenate(blocks, axis=0))
            both = product_nt(c_left, jnp.concatenate([high, low, high], axis=1))
            res, ims = [], []
            for n in range(len(fields)):
                from_re = both[:, n * 256 : n * 256 + LANES]
                from_im = both[:, n * 256 + LANES : n * 256 + 256]
                res.append(from_re[:16] - from_im[16:])
                ims.append(from_im[:16] + from_re[16:])
            spectra.append((jnp.concatenate(res, axis=0), jnp.concatenate(ims, axis=0)))
        return inverse_lines(spectra, ti)

    def weigh(images, count, out):
        for a in range(4):
            map_re, map_im = picked[2 * a], picked[2 * a + 1]
            for n in range(count):
                re = images[a][0][n * 16 : (n + 1) * 16]
                im = images[a][1][n * 16 : (n + 1) * 16]
                row = n * 8 + 2 * a
                out[pl.ds(row, 16, stride=16), :] = map_re * re + map_im * im
                out[pl.ds(row + 1, 16, stride=16), :] = map_re * im - map_im * re

    pick = outward[32:48, :].astype(BF16)
    for plane in range(8):
        split = three(turned_maps[plane])
        picked[plane] = (
            product(pick, split[:, :LANES])
            + product(pick, split[:, LANES : 2 * LANES])
            + product(pick, split[:, 2 * LANES :])
        )
    for a in range(4):
        power = picked[2 * a] * picked[2 * a] + picked[2 * a + 1] * picked[2 * a + 1]
        partial_out[pl.ds(8 + 2 * a, 16, stride=16), :] = power
        partial_out[pl.ds(9 + 2 * a, 16, stride=16), :] = power
    loads[5].wait()
    weigh(to_images((0,)), 1, partial_out)

    for load in loads[6:8]:
        load.wait()
    hidden[0:64, 0:LANES] = jnp.zeros((64, LANES), F32)
    for tap in range(18):
        hidden[tap : tap + 1, 0:64] = first_in[tap]
        hidden[32 + tap : 33 + tap, 0:64] = second_in[tap]
    row24 = lax.broadcasted_iota(jnp.int32, (24, LANES), 0)
    weights[g] = jnp.where(
        row24 < 18,
        hidden[0:24, 0:LANES] + pltpu.roll(hidden[32:56, 0:LANES], 64, 1),
        jnp.full((24, LANES), size_ref[0], F32),
    )

    pl.semaphore_wait(barrier, 32)

    def block_of(at_k):
        q = lax.rem(at_k, 2) * 8 + lax.div(at_k, 2)
        return pl.ds(pl.multiple_of(q * 16, 16), 16)

    for at_g, at_k, _ in receivers:
        send(
            partial_out.at[block_of(at_k)], partial_land.at[k], part_send, part_recv,
            place(at_g, at_k),
        )
    partial_land[k] = partial_out[block_of(k), :]
    for at_g in segment_peers:
        send(weights.at[g], weights.at[g], pack_send, pack_recv, place(at_g, k))
    for at_g, at_k, at_core in receivers:
        send(maps_out.at[at_core], maps_land.at[k], maps_send, maps_recv, place(at_g, at_k))

    loads[8].wait()
    for part in range(2):
        masked[1, part] = cotangent[part]
        masked[2, part] = cotangent[part] * sampled[...]
    weigh(to_images((1, 2)), 2, ending_out)
    for at_g, at_k, _ in receivers:
        send(
            ending_out.at[block_of(at_k)], ending_land.at[k], end_send, end_recv,
            place(at_g, at_k),
        )
    ending_land[k] = ending_out[block_of(k), :]

    for load in loads[9:]:
        load.wait()
    g_high, g_low = parts(gc[...])
    g_left = jnp.concatenate([g_high, g_low], axis=1)
    for m in range(4):
        spots_m = padded(sampled[pl.ds(m, QUARTER, stride=4), :]).astype(BF16)
        rows = product_nt(g_left, jnp.concatenate([spots_m, spots_m], axis=1))
        lattice[m, 0] = rows[:16]
        lattice[m, 1] = rows[16:]

    def cascade_of(step):
        return jnp.where(step < CASC, step, STEPS - 1 - step)

    def step_size(cascade):
        return weights[cascade, 18:19, :]

    def prepare(step):
        way = (step >= CASC).astype(jnp.int32)
        raw = weights[cascade_of(step)]
        lane = lax.broadcasted_iota(jnp.int32, raw.shape, 1)
        turned = pltpu.roll(raw, 64, 1)
        first = jnp.where(lane < 64, raw, turned)
        second = jnp.where(lane < 64, turned, raw)
        enter = jnp.where(way == 0, first, second)
        leave = jnp.where(way == 0, second, first)

        def columns(values):
            high = values.astype(BF16).astype(F32)
            return jnp.concatenate([high, values - high, jnp.zeros((80, LANES), F32)], axis=0)

        flat = columns(enter).T[:64].astype(BF16)
        spread = product(flat, expand[way]).astype(BF16)
        for a in range(4):
            w_in[a * 64 : (a + 1) * 64, :] = spread[:, a * 256 : (a + 1) * 256]
        tall = product(choose[way], columns(leave).astype(BF16))
        inside = (
            jnp.where(w > 0, 1.0, 0.0), jnp.float32(1.0), jnp.where(w < WIDTH - 1, 1.0, 0.0)
        )
        for j in range(3):
            block = tall[j * 64 : (j + 1) * 64]
            left = block * misc[320:384] * inside[j]
            right = block * misc[384:448] * inside[j]
            w_out[:, j * 256 : j * 256 + LANES] = left.astype(BF16)
            w_out[:, j * 256 + LANES : (j + 1) * 256] = right.astype(BF16)

    finish(weights.at[pl.ds(0, WIDTH - 1)], pack_recv)
    prepare(jnp.int32(0))

    def near(step):
        for distance in (2, -2, 1, -1):
            send(
                state.at[step, 2], state.at[step, 2 - distance],
                near_send.at[step], near_recv.at[step],
                role(lax.rem(w + distance + WIDTH, WIDTH), s),
            )

    def far(step, displacements):
        for displacement in displacements:
            send(
                gathered.at[step, s], gathered.at[step, s],
                far_send.at[step],
                far_late.at[step] if displacement[0] == 2 else far_recv.at[step],
                around(displacement),
            )

    finish(partial_land.at[pl.ds(0, COILS - 1)], part_recv)
    total = partial_land[0]
    for n in range(1, COILS):
        total = total + partial_land[n]
    state[0, 2] = total[0:8]
    near(0)
    energy[...] = total[8:16]
    memory[...] = jnp.zeros_like(memory)
    sums[...] = jnp.zeros_like(sums)
    q_plain[...] = jnp.zeros_like(q_plain)
    q_masked[...] = jnp.zeros_like(q_masked)

    def normal(step):
        v = [[jnp.zeros((16, LANES), F32)] * 2 for _ in range(4)]
        for blocks, count, sem in (((0, 1, 2), 11, far_recv), ((3,), 4, far_late)):
            finish(gathered.at[step, pl.ds(0, count)], sem.at[step])
            for block in blocks:
                row = lax.rem(y + ROWS[block], 4)
                p = []
                for a in range(4):
                    res, ims = [], []
                    for inner in range(4):
                        other = row * 4 + inner
                        re = gathered[step, other, 2 * a : 2 * a + 1, :]
                        im = gathered[step, other, 2 * a + 1 : 2 * a + 2, :]
                        span = pl.ds(pl.multiple_of(other * 16, 16), 16)
                        map_re = maps_all[2 * a, span, :]
                        map_im = maps_all[2 * a + 1, span, :]
                        res.append(map_re * re - map_im * im)
                        ims.append(map_re * im + map_im * re)
                    p.append((jnp.concatenate(res, axis=0), jnp.concatenate(ims, axis=0)))
                residues = quarters_to_residues(p)
                for m in range(4):
                    spectrum[m, pl.ds(block * 64, 64), :] = triple(*residues[m])
            start, size = blocks[0] * 64, len(blocks) * 64
            for m in range(4):
                lines = product(spectrum[m, pl.ds(start, size), :], tf(m))
                re, im = v[m]
                for n in range(size // 16):
                    other = start // 16 + n
                    g_re = lattice[m, 0, other : other + 1, :]
                    g_im = lattice[m, 1, other : other + 1, :]
                    x_re = lines[n * 16 : (n + 1) * 16, :LANES]
                    x_im = lines[n * 16 : (n + 1) * 16, LANES:]
                    re = re + (g_re * x_re - g_im * x_im)
                    im = im + (g_re * x_im + g_im * x_re)
                v[m] = [re, im]
        back = inverse_lines(v, ti)
        rows = []
        mine = pl.ds(pl.multiple_of(s * 16, 16), 16)
        for a in range(4):
            map_re, map_im = maps_all[2 * a, mine, :], maps_all[2 * a + 1, mine, :]
            rows.append(jnp.sum(map_re * back[a][0] + map_im * back[a][1], axis=0, keepdims=True))
            rows.append(jnp.sum(map_re * back[a][1] - map_im * back[a][0], axis=0, keepdims=True))
        return jnp.concatenate(rows, axis=0)

    def arrived(step):
        finish(gathered.at[step, pl.ds(0, 11)], far_recv.at[step])
        finish(gathered.at[step, pl.ds(0, 4)], far_late.at[step])

    def accumulate(older):
        memory[...] = memory[...] * (1.0 - step_size(cascade_of(older))) + normal(older)

    def surroundings(step):
        finish(state.at[step, pl.ds(0, 4)], near_recv.at[step])
        taps = []
        for column in range(5):
            at_w = w + (column - 2)
            tile = state[step, column]
            if column != 2:
                tile = jnp.where((at_w >= 0) & (at_w < WIDTH), tile, jnp.zeros_like(tile))
            before, after = shifted(tile)
            taps += [before, tile, after]
        return jnp.concatenate(taps, axis=0)

    def enter(taps):
        high = taps.astype(BF16).astype(F32)
        low = taps - high
        rest = jnp.zeros((40, LANES), F32)
        columns = []
        for j in range(3):
            span = slice(24 * j, 24 * j + 72)
            columns.append(jnp.concatenate([high[span], low[span], high[span], rest], axis=0))
        return product(w_in[...], jnp.concatenate(columns, axis=1).astype(BF16))

    def leave(step, values):
        stack = jnp.concatenate([values[:, j * LANES : (j + 1) * LANES] for j in range(3)], axis=0)
        stack_high, stack_low = parts(stack)
        first = product(w_out[...], stack_high)
        second = product(w_out[0:32, :], stack_low)
        response = first[0:24] + first[32:56] + second[0:24]
        before, _ = shifted(response[0:8])
        _, after = shifted(response[16:24])
        gathered[step, s] = before + response[8:16] + after

    def activate(cascade, taps):
        before = enter(taps)
        gate = 1.0 / (1.0 + jnp.exp(-before))
        after = before * gate
        slope[cascade] = gate + after * (1.0 - gate)
        centre[cascade] = after[:, LANES : 2 * LANES]
        taps_saved[cascade] = taps[24:96]
        return after

    def advance(step):
        state[step + 1, 2] = (
            state[step, 2] - step_size(cascade_of(step)) * memory[...]
            + energy[...] * gathered[step, s]
        )
        near(step + 1)

    def forward(step, carry):
        leave(step, activate(step, surroundings(step)))

        @pl.when(step < CASC - 2)
        def _():
            far(step, AROUND[:LONG])

        @pl.when(step == 1)
        def _():
            finish(maps_land.at[pl.ds(0, COILS - 1)], maps_recv)
            for coil in range(COILS):
                block = padded(maps_land[coil]).T
                for plane in range(8):
                    maps_all[plane, pl.ds(coil, SLICES, stride=16), :] = block[
                        plane * SLICES : (plane + 1) * SLICES
                    ]

        @pl.when(step >= 1)
        def _():
            accumulate(step - 1)

        advance(step)

        @pl.when(step < CASC - 2)
        def _():
            far(step, AROUND[LONG:])

        @pl.when(step == 2)
        def _():
            finish(ending_land.at[pl.ds(0, COILS - 1)], end_recv)
            total = ending_land[0]
            for n in range(1, COILS):
                total = total + ending_land[n]
            state[CASC, 2] = total[0:8]
            near(CASC)
            final[...] = total[8:16]

        sums[step + 1] = sums[step] * (1.0 - step_size(step)) + gathered[step, s]
        prepare(step + 1)
        return carry

    lax.fori_loop(0, CASC - 1, forward, jnp.int32(0))
    activate(CASC - 1, surroundings(CASC - 1))
    prepare(jnp.int32(CASC))
    memory[...] = final[...]

    def filter_grads(cascade, taps):
        grads = []
        pairs = (
            (hidden[:, LANES : 2 * LANES], taps_saved[cascade]),
            (centre[cascade], taps),
        )
        for values, near_taps in pairs:
            left_high, left_low = parts(values)
            right = jnp.concatenate([near_taps, jnp.zeros((56, LANES), F32)], axis=0)
            right_high, right_low = parts(right)
            full = product_nt(
                jnp.concatenate([left_high, left_low, left_high], axis=1),
                jnp.concatenate([right_high, right_high, right_low], axis=1),
            ) * misc[64:320]
            grads.append(full[0:64] + full[64:128] + full[128:192] + full[192:256])
        fold = misc[16:64].astype(BF16)
        folded = product_nt(
            jnp.concatenate([fold, fold, fold], axis=1), three(jnp.concatenate(grads, axis=0))
        )
        lanes = lax.broadcasted_iota(jnp.int32, (24, LANES), 1)
        sizes = -jnp.sum(sums[cascade] * memory[...], axis=0, keepdims=True)
        w_send[cascade] = jnp.where(
            row24 == 18, sizes, jnp.where(lanes < 64, folded[0:24], folded[24:48])
        )

        @pl.when(g == cascade)
        def _():
            w_land[g] = w_send[cascade]

        @pl.when(g != cascade)
        def _():
            send(
                w_send.at[cascade], w_land.at[g], ws_send.at[cascade], ws_recv, place(cascade, k)
            )

    def collect(cascade):
        keep = 1.0 - step_size(cascade)
        slot = STEPS - 1 - cascade
        images = gathered[slot].reshape(SLICES * 8, LANES)
        q_plain[...] = q_plain[...] + images
        q_masked[...] = q_masked[...] * keep + images
        target = jnp.where((cascade == 1) & (x_lo == 0), 0, cascade)

        @pl.when(lax.rem(target, 2) == x_lo)
        def _():
            q_out[cascade, 0] = q_plain[...].T[:QUARTER]
            q_out[cascade, 1] = q_masked[...].T[:QUARTER]

            @pl.when(g == target)
            def _():
                q_land[z] = q_out[cascade]

            @pl.when(g != target)
            def _():
                send(q_out.at[cascade], q_land.at[z], q_send, q_recv, place(target, k))

    def backward(step, carry):
        cascade = STEPS - 1 - step
        taps = surroundings(step)
        values = enter(taps) * slope[cascade]
        hidden[...] = values
        leave(step, values)
        taps_saved[CASC] = taps[24:96]
        ending = step == STEPS - 1

        @pl.when(jnp.logical_not(ending))
        def _():
            far(step, AROUND[:LONG])

        @pl.when(ending)
        def _():
            @pl.when(z == 0)
            def _():
                tail_land[0] = gathered[step, s]

            @pl.when(z != 0)
            def _():
                send(
                    gathered.at[step, s], tail_land.at[z], tail_send, tail_recv, place(x_lo, k)
                )

        @pl.when((step > CASC) & (step < STEPS - 1))
        def _():
            accumulate(step - 1)

        @pl.when(step < STEPS - 1)
        def _():
            advance(step)

        @pl.when(jnp.logical_not(ending))
        def _():
            far(step, AROUND[LONG:])
            prepare(step + 1)

        filter_grads(cascade, taps_saved[CASC])

        @pl.when(step == STEPS - 1)
        def _():
            arrived(step - 1)

        @pl.when(step > CASC)
        def _():
            collect(cascade + 1)

        return carry

    lax.fori_loop(CASC, STEPS, backward, jnp.int32(0))

    even = [(dy, x_at) for dy in (2, 1, 3, 0) for x_at in (0, 2)]

    @pl.when(z == 0)
    def _():
        finish(tail_land.at[pl.ds(0, 3)], tail_recv)
        for dy, x_at in even:
            at_s = 4 * lax.rem(y + dy, 4) + x_at

            @pl.when(at_s == s)
            def _():
                late_land[core, s] = tail_land[...]

            @pl.when(at_s != s)
            def _():
                send(
                    tail_land, late_land.at[core, s], late_send, late_recv, role(core, at_s)
                )

    finish(w_land.at[pl.ds(0, WIDTH - 1)], ws_recv)
    total = w_land[0]
    for n in range(1, WIDTH):
        total = total + w_land[n]
    w_pair[core] = total
    send(w_pair.at[core], w_pair.at[core], wp_send, wp_recv, place(g, 2 * pair + 1 - core))

    def spread_out(count, image_of, into):
        p = []
        for a in range(4):
            columns = [
                [
                    turned_maps[2 * a + part, pl.ds(at_w, SLICES, stride=WIDTH), :]
                    for at_w in range(WIDTH)
                ]
                for part in range(2)
            ]
            map_re = jnp.concatenate(columns[0], axis=0)
            map_im = jnp.concatenate(columns[1], axis=0)
            res, ims = [], []
            for image in range(count):
                re = image_of(image, 2 * a)
                im = image_of(image, 2 * a + 1)
                res.append(map_re * re - map_im * im)
                ims.append(map_re * im + map_im * re)
            p.append((jnp.concatenate(res, axis=0), jnp.concatenate(ims, axis=0)))
        residues = quarters_to_residues(p)
        for m in range(4):
            lines = product_nt(tft[m], triple(*residues[m]))
            fields = []
            for image in range(count):
                span = slice(image * LANES, (image + 1) * LANES)
                field = product(
                    triple(lines[0:QUARTER, span], lines[LANES : LANES + QUARTER, span]), dz()
                )
                fields.append((field[:, :LANES], field[:, LANES:]))
            into(pl.ds(m, QUARTER, stride=4), fields)

    keep = jnp.ones((1, LANES), F32)
    for cascade in range(CASC):
        factor = 1.0 - step_size(cascade)
        keep = jnp.where(cascade >= g, keep * factor, keep)
    late_factor = jnp.where(g == 0, 1.0 - step_size(0), jnp.ones((1, LANES), F32))

    finish(w_pair.at[0], wp_recv)
    w_all[pair] = w_pair[0] + w_pair[1]
    for dy in (2, 1, 3, 0):
        for dx in (2, 0):
            if dy or dx:
                send(
                    w_all.at[pair], w_all.at[pair], wa_send, wa_recv, around((dy, dx))
                )

    partner = place(g, 2 * pair + 1 - core)
    finish(q_land.at[pl.ds(0, 3)], q_recv)
    for at_z in range(4):
        for image in range(2):
            q_open[core, at_z, image] = padded(q_land[at_z, image]).T
    send(q_open.at[core], q_open.at[core], pass_send.at[0], pass_recv.at[0], partner)
    finish(q_open.at[0], pass_recv.at[0])

    def early(image, plane):
        return jnp.concatenate(
            [
                q_open[n % 2, n // 2, image, pl.ds(plane, SLICES, stride=8), :]
                for n in range(WIDTH)
            ],
            axis=0,
        )

    def first_part(rows, fields):
        on = sampled[rows, :] > 0.5
        for part in range(2):
            seed = cotangent[part, rows, :]
            grad_k[part, rows, :] = jnp.where(
                on, keep * seed + late_factor * fields[1][part], seed + fields[0][part]
            )

    spread_out(2, early, first_part)

    @pl.when(g == 0)
    def _():
        finish(late_land.at[0, pl.ds(0, SLICES - 1)], late_recv)
        send(late_land.at[core], late_land.at[core], pass_send.at[1], pass_recv.at[1], partner)
        finish(late_land.at[0], pass_recv.at[1])

        def late(image, plane):
            return jnp.concatenate(
                [late_land[n % 2, :, n // 2, plane, :] for n in range(WIDTH)], axis=0
            )

        def second_part(rows, fields):
            for part in range(2):
                grad_k[part, rows, :] = grad_k[part, rows, :] + fields[0][part]

        spread_out(1, late, second_part)

    finish(w_all.at[pl.ds(0, 7)], wa_recv)
    total = w_all[0]
    for n in range(1, 8):
        total = total + w_all[n]
    for tap in range(18):
        grad_w[tap] = total[tap : tap + 1]
    grad_w[18] = jnp.broadcast_to(jnp.sum(total[18:19], axis=1, keepdims=True), (1, LANES))

    finish(weights.at[pl.ds(0, WIDTH - 1)], pack_send)
    finish(partial_land.at[pl.ds(0, COILS - 1)], part_send)
    finish(ending_land.at[pl.ds(0, COILS - 1)], end_send)
    finish(maps_land.at[pl.ds(0, COILS - 1)], maps_send)
    finish(w_pair.at[0], wp_send)
    finish(w_all.at[pl.ds(0, 7)], wa_send)
    finish(q_land.at[pl.ds(0, 3)], q_send)
    finish(q_open.at[0], pass_send.at[0])

    @pl.when(z != 0)
    def _():
        finish(tail_land.at[0], tail_send)

    @pl.when((z == 0) & (x_lo == 1))
    def _():
        finish(late_land.at[0, pl.ds(0, 8)], late_send)

    @pl.when(g == 0)
    def _():
        finish(late_land.at[0, pl.ds(0, 7)], late_send)
        finish(late_land.at[0], pass_send.at[1])

    def drain(step, carry):
        @pl.when((step < CASC - 2) | ((step >= CASC) & (step < STEPS - 1)))
        def _():
            finish(gathered.at[step, pl.ds(0, COILS - 1)], far_send.at[step])

        finish(state.at[step, pl.ds(0, 4)], near_send.at[step])

        @pl.when((step < CASC) & (step != g))
        def _():
            finish(w_send.at[lax.rem(step, CASC)], ws_send.at[lax.rem(step, CASC)])

        return carry

    lax.fori_loop(0, STEPS, drain, jnp.int32(0))


def shards(measured, maps, mask, first_filters, second_filters, step_sizes, cotangent):
    tables = [jnp.asarray(table) for table in constants()]
    dma = pltpu.SemaphoreType.DMA
    field = pltpu.VMEM((2, LINES, LANES), F32)
    scratch = [
        field, field, field,
        pltpu.VMEM((SLICES, LINES), jnp.int32),
        pltpu.VMEM((18, 1, HIDDEN), F32),
        pltpu.VMEM((18, 1, HIDDEN), F32),
    ]
    whole_tables = tables[:5]
    scratch += [pltpu.VMEM(table.shape, table.dtype) for table in whole_tables]
    scratch += [
        pltpu.VMEM((48, LANES), F32),
        pltpu.VMEM((32, LANES), F32),
        dma((13,)),
        pltpu.VMEM((LINES, LANES), F32),
        pltpu.VMEM((3, 2, LINES, LANES), F32),
        pltpu.VMEM((8, LANES, LANES), F32),
        pltpu.VMEM((2, QUARTER, LANES), F32),
        pltpu.VMEM((COILS, QUARTER, LANES), F32),
        pltpu.VMEM((8, SLICES * COILS, LANES), F32),
        pltpu.VMEM((4, 2, SLICES, LANES), F32),
        pltpu.VMEM((8, SLICES, LANES), F32),
        pltpu.VMEM((SLICES * 16, LANES), F32),
        pltpu.VMEM((COILS, 16, LANES), F32),
        pltpu.VMEM((SLICES * 16, LANES), F32),
        pltpu.VMEM((COILS, 16, LANES), F32),
        pltpu.VMEM((CASC, 24, LANES), F32),
        pltpu.VMEM((256, 256), BF16),
        pltpu.VMEM((64, 768), BF16),
        pltpu.VMEM((STEPS, 5, 8, LANES), F32),
        pltpu.VMEM((STEPS, SLICES, 8, LANES), F32),
        pltpu.VMEM((CASC, 256, 3 * LANES), F32),
        pltpu.VMEM((CASC, 256, LANES), F32),
        pltpu.VMEM((CASC + 1, 72, LANES), F32),
        pltpu.VMEM((256, 3 * LANES), F32),
        pltpu.VMEM((4, 256, 768), BF16),
        pltpu.VMEM((8, LANES), F32),
        pltpu.VMEM((8, LANES), F32),
        pltpu.VMEM((8, LANES), F32),
        pltpu.VMEM((CASC, 8, LANES), F32),
        pltpu.VMEM((SLICES * 8, LANES), F32),
        pltpu.VMEM((SLICES * 8, LANES), F32),
        pltpu.VMEM((CASC, 2, QUARTER, LANES), F32),
        pltpu.VMEM((4, 2, QUARTER, LANES), F32),
        pltpu.VMEM((2, 4, 2, SLICES * 8, LANES), F32),
        pltpu.VMEM((4, 8, LANES), F32),
        pltpu.VMEM((2, SLICES, 4, 8, LANES), F32),
        pltpu.VMEM((CASC, 24, LANES), F32),
        pltpu.VMEM((WIDTH, 24, LANES), F32),
        pltpu.VMEM((2, 24, LANES), F32),
        pltpu.VMEM((8, 24, LANES), F32),
        dma, dma, dma, dma, dma, dma, dma, dma,
        dma((STEPS,)), dma((STEPS,)), dma((STEPS,)), dma((STEPS,)), dma((STEPS,)),
        dma, dma, dma, dma, dma, dma, dma((2,)), dma((2,)),
        dma((CASC,)), dma, dma, dma, dma, dma,
    ]
    there = pl.BlockSpec(memory_space=pltpu.HBM)
    whole = pl.BlockSpec(memory_space=pltpu.VMEM)
    first = jnp.transpose(first_filters, (2, 0, 1))
    second = jnp.transpose(second_filters, (1, 0, 2))
    operands = [measured[0], maps[0], cotangent[0], mask, first, second]
    grad_k, grad_w = pl.pallas_call(
        kernel,
        out_shape=[
            jax.ShapeDtypeStruct((2, LINES, LANES), F32),
            jax.ShapeDtypeStruct((19, 1, LANES), F32),
        ],
        in_specs=[there] * 6 + [pl.BlockSpec(memory_space=pltpu.SMEM)] + [there] * len(tables),
        out_specs=[whole, whole],
        scratch_shapes=scratch,
        compiler_params=pltpu.CompilerParams(
            collective_id=0, has_side_effects=True, vmem_limit_bytes=58 * 1024 * 1024
        ),
        name="cascades",
    )(*operands, step_sizes, *tables)
    first = jnp.transpose(grad_w[:18, :, :64], (1, 2, 0))
    second = jnp.transpose(grad_w[:18, :, 64:], (1, 0, 2))
    return grad_k[None, None], first, second, grad_w[18, 0, :1]


def solution(mesh):
    in_specs = (
        P("coil", None, None, None),
        P("coil", None, None, None),
        P(),
        P("segment", None, None),
        P("segment", None, None),
        P("segment"),
        P("coil", None, None, None),
    )
    out_specs = (
        P("segment", "coil", None, None, None),
        P("segment", None, None),
        P("segment", None, None),
        P("segment"),
    )
    return jax.shard_map(shards, mesh=mesh, in_specs=in_specs, out_specs=out_specs, check_vma=False)
```

```python
import functools

import jax
import jax.numpy as jnp
import ml_dtypes
import numpy as np
from jax import lax
from jax.experimental import pallas as pl
from jax.experimental.pallas import tpu as pltpu
from jax.sharding import PartitionSpec as P

F32 = jnp.float32
BF16 = jnp.bfloat16
LINES = 320
QUARTER = 80
LANES = 128
WIDTH = 8
SLICES = 16
COILS = 16
CASC = 8
STEPS = 2 * CASC
HIDDEN = 64
MESH = pl.DeviceIdType.MESH
AROUND = sorted(
    [(dy, dx) for dy in range(4) for dx in range(4) if dy or dx],
    key=lambda d: -(min(d[0], 4 - d[0]) + min(d[1], 4 - d[1])),
)
LONG = 11
ROWS = (0, 1, 3, 2)


def stacked(table):
    high = table.astype(ml_dtypes.bfloat16)
    low = (table - high.astype(np.float64)).astype(ml_dtypes.bfloat16)
    return np.concatenate([high, high, low], axis=-2)


@functools.lru_cache(maxsize=None)
def constants():
    forward = np.zeros((4, 256, 256))
    inverse = np.zeros((4, 256, 256))
    v = np.arange(QUARTER)[:, None]
    b = np.arange(QUARTER)[None, :]
    re, im = slice(0, QUARTER), slice(LANES, LANES + QUARTER)
    for m in range(4):
        angle = 2 * np.pi * (((4 * v + m) * b) % LINES) / LINES
        cosine = np.cos(angle) / np.sqrt(LINES)
        sine = np.sin(angle) / np.sqrt(LINES)
        forward[m, re, re] = cosine.T
        forward[m, re, im] = -sine.T
        forward[m, im, re] = sine.T
        forward[m, im, im] = cosine.T
        inverse[m, re, re] = cosine
        inverse[m, re, im] = sine
        inverse[m, im, re] = -sine
        inverse[m, im, im] = cosine
    tf = stacked(forward)
    ti = stacked(inverse)
    tft = np.ascontiguousarray(np.swapaxes(tf, 1, 2))

    dz = np.zeros((256, 256))
    for w in range(WIDTH):
        for s in range(SLICES):
            for kz in range(SLICES):
                angle = 2 * np.pi * (s * kz % SLICES) / SLICES
                row, lane = w * SLICES + s, kz * WIDTH + w
                dz[row, lane] = np.cos(angle) / 4
                dz[row, LANES + lane] = -np.sin(angle) / 4
                dz[LANES + row, lane] = np.sin(angle) / 4
                dz[LANES + row, LANES + lane] = np.cos(angle) / 4
    dz = stacked(dz)

    rep = np.zeros((SLICES, LANES), np.float32)
    for kz in range(SLICES):
        rep[kz, kz * WIDTH : (kz + 1) * WIDTH] = 1
    outward = np.zeros((16, 48, LANES), np.float32)
    for g in range(WIDTH):
        for x_hi in range(2):
            for q in range(16):
                j = q % 8
                s = 2 * j + (g % 2 if j % 2 == x_hi else 1 - g % 2)
                w = 2 * (g // 2) + q // 8
                outward[2 * g + x_hi, 32 + q, s * WIDTH + w] = 1
                for kz in range(SLICES):
                    angle = 2 * np.pi * (s * kz % SLICES) / SLICES
                    outward[2 * g + x_hi, q, kz * WIDTH + w] = np.cos(angle) / 4
                    outward[2 * g + x_hi, 16 + q, kz * WIDTH + w] = np.sin(angle) / 4
    gc = np.zeros((SLICES, 32, LANES), np.float32)
    for kz in range(SLICES):
        for s in range(SLICES):
            for n in range(SLICES):
                other = 4 * ((s // 4 + ROWS[n // 4]) % 4) + n % 4
                angle = 2 * np.pi * ((s - other) * kz % SLICES) / SLICES
                gc[s, n, kz * WIDTH] = np.cos(angle) / 16
                gc[s, 16 + n, kz * WIDTH] = np.sin(angle) / 16

    expand = np.zeros((2, LANES, 4 * 256), np.float32)
    choose = np.zeros((2, 3 * 64, LANES), np.float32)
    fold = np.zeros((2, 24, LANES), np.float32)
    amask = np.zeros((64, 256), np.float32)
    gmask = np.zeros((256, LANES), np.float32)
    for ch in range(2):
        for dh in range(3):
            for dw in range(3):
                taps = (ch * 9 + dh * 3 + dw, ch * 9 + (2 - dh) * 3 + (2 - dw))
                for way in range(2):
                    for a in range(4):
                        lane = dw * 24 + dh * 8 + a * 2 + ch
                        expand[way, taps[way], a * 256 + lane] = 1
                        expand[way, taps[way], a * 256 + 72 + lane] = 1
                        expand[way, 24 + taps[way], a * 256 + 144 + lane] = 1
                        fold[way, taps[way], lane] = 1
                        for hl in range(2):
                            row = hl * 32 + dh * 8 + a * 2 + ch
                            choose[way, dw * 64 + row, hl * 24 + taps[way]] = 1
                            amask[row, a * 64 : (a + 1) * 64] = 1
                        gmask[a * 64 : (a + 1) * 64, lane] = 1
    bf = ml_dtypes.bfloat16
    wide = np.concatenate([tf.reshape(-1, 256), ti.reshape(-1, 256), dz], axis=0)
    misc = np.concatenate(
        [rep, fold.reshape(48, LANES), gmask, amask[:, :LANES], amask[:, LANES:]], axis=0
    )
    return wide, tft, expand.astype(bf), choose.astype(bf), misc, outward, gc


def product(left, right):
    return jnp.dot(left, right, preferred_element_type=F32)


def product_nt(left, right):
    return lax.dot_general(left, right, (((1,), (1,)), ((), ())), preferred_element_type=F32)


def parts(values):
    high = values.astype(BF16)
    low = (values - high.astype(F32)).astype(BF16)
    return high, low


def three(values):
    first = values.astype(BF16)
    rest = values - first.astype(F32)
    second = rest.astype(BF16)
    third = (rest - second.astype(F32)).astype(BF16)
    return jnp.concatenate([first, second, third], axis=1)


def triple(re, im):
    re_high, re_low = parts(re)
    im_high, im_low = parts(im)
    return jnp.concatenate([re_high, im_high, re_low, im_low, re_high, im_high], axis=1)


def shifted(tile):
    lane = lax.broadcasted_iota(jnp.int32, (8, LANES), 1)
    row = lax.broadcasted_iota(jnp.int32, (8, LANES), 0)
    zero = jnp.zeros_like(tile)
    last = QUARTER - 1
    next_first = pltpu.roll(pltpu.roll(tile, last, 1), 6, 0)
    after = jnp.where(
        lane < last,
        pltpu.roll(tile, LANES - 1, 1),
        jnp.where((lane == last) & (row < 6), next_first, zero),
    )
    previous_last = pltpu.roll(pltpu.roll(tile, LANES - last, 1), 2, 0)
    before = jnp.where(
        (lane >= 1) & (lane < QUARTER),
        pltpu.roll(tile, 1, 1),
        jnp.where((lane == 0) & (row >= 2), previous_last, zero),
    )
    return before, after


def quarters_to_residues(p):
    t0 = [p[0][k] + p[2][k] for k in range(2)]
    t1 = [p[0][k] - p[2][k] for k in range(2)]
    t2 = [p[1][k] + p[3][k] for k in range(2)]
    t3 = [p[1][k] - p[3][k] for k in range(2)]
    return (
        (t0[0] + t2[0], t0[1] + t2[1]),
        (t1[0] + t3[1], t1[1] - t3[0]),
        (t0[0] - t2[0], t0[1] - t2[1]),
        (t1[0] - t3[1], t1[1] + t3[0]),
    )


def residues_to_quarters(z):
    t0 = [z[0][k] + z[2][k] for k in range(2)]
    t1 = [z[0][k] - z[2][k] for k in range(2)]
    t2 = [z[1][k] + z[3][k] for k in range(2)]
    t3 = [z[1][k] - z[3][k] for k in range(2)]
    return (
        (t0[0] + t2[0], t0[1] + t2[1]),
        (t1[0] - t3[1], t1[1] + t3[0]),
        (t0[0] - t2[0], t0[1] - t2[1]),
        (t1[0] + t3[1], t1[1] - t3[0]),
    )


def inverse_lines(v, table):
    z = []
    for m in range(4):
        result = product(triple(*v[m]), table(m))
        z.append((result[:, :LANES], result[:, LANES:]))
    return residues_to_quarters(z)


def kernel(
    measured_hbm, maps_hbm, cotangent_hbm, mask_hbm, first_hbm, second_hbm, size_ref,
    wide_hbm, tft_hbm, expand_hbm, choose_hbm, misc_hbm, outward_hbm, gc_hbm,
    grad_k, grad_w,
    measured, maps, cotangent, mask, first_in, second_in,
    wide, tft, expand, choose, misc, outward, gc, load_sem,
    sampled, masked, turned_maps, maps_out, maps_land, maps_all, lattice, picked, partial_out, partial_land,
    ending_out, ending_land,
    weights, w_in, w_out, state, gathered, slope, centre, taps_saved, hidden, spectrum,
    energy, memory, final, sums, q_plain, q_masked, q_out, q_land, q_open, tail_land, late_land,
    w_send, w_land, w_pair, w_all,
    pack_send, pack_recv, part_send, part_recv, end_send, end_recv, maps_send, maps_recv,
    near_send, near_recv, far_send, far_recv, far_late, q_send, q_recv,
    tail_send, tail_recv, late_send, late_recv, pass_send, pass_recv,
    ws_send, ws_recv, wp_send, wp_recv, wa_send, wa_recv,
):
    g = lax.axis_index("segment")
    k = lax.axis_index("coil")
    z, x_lo = lax.div(g, 2), lax.rem(g, 2)
    pair, core = lax.div(k, 2), lax.rem(k, 2)
    y, x_hi = lax.div(pair, 2), lax.rem(pair, 2)
    w = 2 * z + core
    s = 2 * pair + x_lo
    x = 2 * x_hi + x_lo

    def role(at_w, at_s):
        return {
            "segment": 2 * lax.div(at_w, 2) + lax.rem(at_s, 2),
            "coil": 2 * lax.div(at_s, 2) + lax.rem(at_w, 2),
        }

    def around(displacement):
        dy, dx = displacement
        return role(w, 4 * lax.rem(y + dy, 4) + lax.rem(x + dx, 4))

    def place(at_g, at_k):
        return {"segment": at_g, "coil": at_k}

    receivers = []
    for dy in (2, 1, 3, 0):
        for flip in range(2):
            for at_core in range(2):
                if dy or flip:
                    at_k = 4 * lax.rem(y + dy, 4) + 2 * lax.rem(x_hi + flip, 2) + at_core
                    at_g = g if flip == 0 else 2 * z + 1 - x_lo
                    receivers.append((at_g, at_k, at_core))
    receivers.append((g, 2 * pair + 1 - core, 1 - core))
    segment_peers = [lax.rem(g + n, WIDTH) for n in range(1, WIDTH)]

    def send(source, target, send_sem, recv_sem, device):
        pltpu.make_async_remote_copy(
            src_ref=source, dst_ref=target, send_sem=send_sem, recv_sem=recv_sem,
            device_id=device, device_id_type=MESH,
        ).start()

    def finish(extent, sem):
        pltpu.make_async_copy(extent, extent, sem).wait()

    loads = (
        (maps_hbm, maps), (measured_hbm, measured), (mask_hbm, mask), (misc_hbm, misc),
        (outward_hbm.at[2 * g + x_hi], outward), (wide_hbm, wide),
        (first_hbm, first_in), (second_hbm, second_in), (cotangent_hbm, cotangent),
        (gc_hbm.at[s], gc), (expand_hbm, expand), (choose_hbm, choose), (tft_hbm, tft),
    )
    loads = [
        pltpu.make_async_copy(source, target, load_sem.at[n])
        for n, (source, target) in enumerate(loads)
    ]
    barrier = pltpu.get_barrier_semaphore()

    def greet(device):
        pl.semaphore_signal(barrier, inc=1, device_id=device, device_id_type=MESH)

    for dy, dx in AROUND:
        if dx:
            other = lax.rem(x + dx, 4)

            @pl.when(other != 3 - x)
            def _():
                greet(role(w, 4 * lax.rem(y + dy, 4) + other))

    for turn in (2, 1, 3):
        at_z = lax.rem(z + turn, 4)
        greet(place(2 * at_z + 1 - x_lo, k))
        for at_core in range(2):
            greet(place(2 * at_z + x_lo, 2 * pair + at_core))
    for at_g, at_k, _ in receivers:
        greet(place(at_g, at_k))
    for load in loads:
        load.start()

    def tf(m):
        return wide[m * 768 : (m + 1) * 768, :]

    def ti(m):
        return wide[3072 + m * 768 : 3072 + (m + 1) * 768, :]

    def dz():
        return wide[6144:6912, :]

    blank = jnp.zeros((LANES - QUARTER, LANES), F32)

    def padded(values):
        return jnp.concatenate([values, blank], axis=0)

    loads[0].wait()
    for part in range(2):
        for a in range(4):
            block = padded(maps[part, a * QUARTER : (a + 1) * QUARTER, :])
            turned_maps[2 * a + part] = block.T
    for at_core in range(2):
        lines = [
            turned_maps[plane, pl.ds(2 * z + at_core, SLICES, stride=WIDTH), :]
            for plane in range(8)
        ]
        maps_out[at_core] = jnp.concatenate(lines, axis=0).T[:QUARTER]
    maps_land[k] = maps_out[core]

    for load in loads[1:5]:
        load.wait()
    sampled[...] = lax.dot_general(
        mask[...].astype(F32), misc[0:16], (((0,), (0,)), ((), ())), preferred_element_type=F32
    )
    spots = sampled[...]
    for part in range(2):
        masked[0, part] = measured[part] * spots
    c_high, c_low = parts(outward[0:32, :])
    c_left = jnp.concatenate([c_high, c_high, c_low], axis=1)

    def to_images(fields):
        spectra = []
        for m in range(4):
            rows = pl.ds(m, QUARTER, stride=4)
            blocks = [padded(masked[field, part, rows, :]) for field in fields for part in range(2)]
            high, low = parts(jnp.concatenate(blocks, axis=0))
            both = product_nt(c_left, jnp.concatenate([high, low, high], axis=1))
            res, ims = [], []
            for n in range(len(fields)):
                from_re = both[:, n * 256 : n * 256 + LANES]
                from_im = both[:, n * 256 + LANES : n * 256 + 256]
                res.append(from_re[:16] - from_im[16:])
                ims.append(from_im[:16] + from_re[16:])
            spectra.append((jnp.concatenate(res, axis=0), jnp.concatenate(ims, axis=0)))
        return inverse_lines(spectra, ti)

    def weigh(images, count, out):
        for a in range(4):
            map_re, map_im = picked[2 * a], picked[2 * a + 1]
            for n in range(count):
                re = images[a][0][n * 16 : (n + 1) * 16]
                im = images[a][1][n * 16 : (n + 1) * 16]
                row = n * 8 + 2 * a
                out[pl.ds(row, 16, stride=16), :] = map_re * re + map_im * im
                out[pl.ds(row + 1, 16, stride=16), :] = map_re * im - map_im * re

    pick = outward[32:48, :].astype(BF16)
    for plane in range(8):
        split = three(turned_maps[plane])
        picked[plane] = (
            product(pick, split[:, :LANES])
            + product(pick, split[:, LANES : 2 * LANES])
            + product(pick, split[:, 2 * LANES :])
        )
    for a in range(4):
        power = picked[2 * a] * picked[2 * a] + picked[2 * a + 1] * picked[2 * a + 1]
        partial_out[pl.ds(8 + 2 * a, 16, stride=16), :] = power
        partial_out[pl.ds(9 + 2 * a, 16, stride=16), :] = power
    loads[5].wait()
    weigh(to_images((0,)), 1, partial_out)

    for load in loads[6:8]:
        load.wait()
    hidden[0:64, 0:LANES] = jnp.zeros((64, LANES), F32)
    for tap in range(18):
        hidden[tap : tap + 1, 0:64] = first_in[tap]
        hidden[32 + tap : 33 + tap, 0:64] = second_in[tap]
    row24 = lax.broadcasted_iota(jnp.int32, (24, LANES), 0)
    weights[g] = jnp.where(
        row24 < 18,
        hidden[0:24, 0:LANES] + pltpu.roll(hidden[32:56, 0:LANES], 64, 1),
        jnp.full((24, LANES), size_ref[0], F32),
    )

    pl.semaphore_wait(barrier, 32)

    def block_of(at_k):
        q = lax.rem(at_k, 2) * 8 + lax.div(at_k, 2)
        return pl.ds(pl.multiple_of(q * 16, 16), 16)

    for at_g, at_k, _ in receivers:
        send(
            partial_out.at[block_of(at_k)], partial_land.at[k], part_send, part_recv,
            place(at_g, at_k),
        )
    partial_land[k] = partial_out[block_of(k), :]
    for at_g in segment_peers:
        send(weights.at[g], weights.at[g], pack_send, pack_recv, place(at_g, k))
    for at_g, at_k, at_core in receivers:
        send(maps_out.at[at_core], maps_land.at[k], maps_send, maps_recv, place(at_g, at_k))

    loads[8].wait()
    for part in range(2):
        masked[1, part] = cotangent[part]
        masked[2, part] = cotangent[part] * sampled[...]
    weigh(to_images((1, 2)), 2, ending_out)
    for at_g, at_k, _ in receivers:
        send(
            ending_out.at[block_of(at_k)], ending_land.at[k], end_send, end_recv,
            place(at_g, at_k),
        )
    ending_land[k] = ending_out[block_of(k), :]

    for load in loads[9:]:
        load.wait()
    g_high, g_low = parts(gc[...])
    g_left = jnp.concatenate([g_high, g_low], axis=1)
    for m in range(4):
        spots_m = padded(sampled[pl.ds(m, QUARTER, stride=4), :]).astype(BF16)
        rows = product_nt(g_left, jnp.concatenate([spots_m, spots_m], axis=1))
        lattice[m, 0] = rows[:16]
        lattice[m, 1] = rows[16:]

    def cascade_of(step):
        return jnp.where(step < CASC, step, STEPS - 1 - step)

    def step_size(cascade):
        return weights[cascade, 18:19, :]

    def prepare(step):
        way = (step >= CASC).astype(jnp.int32)
        raw = weights[cascade_of(step)]
        lane = lax.broadcasted_iota(jnp.int32, raw.shape, 1)
        turned = pltpu.roll(raw, 64, 1)
        first = jnp.where(lane < 64, raw, turned)
        second = jnp.where(lane < 64, turned, raw)
        enter = jnp.where(way == 0, first, second)
        leave = jnp.where(way == 0, second, first)

        def columns(values):
            high = values.astype(BF16).astype(F32)
            return jnp.concatenate([high, values - high, jnp.zeros((80, LANES), F32)], axis=0)

        flat = columns(enter).T[:64].astype(BF16)
        spread = product(flat, expand[way]).astype(BF16)
        for a in range(4):
            w_in[a * 64 : (a + 1) * 64, :] = spread[:, a * 256 : (a + 1) * 256]
        tall = product(choose[way], columns(leave).astype(BF16))
        inside = (
            jnp.where(w > 0, 1.0, 0.0), jnp.float32(1.0), jnp.where(w < WIDTH - 1, 1.0, 0.0)
        )
        for j in range(3):
            block = tall[j * 64 : (j + 1) * 64]
            left = block * misc[320:384] * inside[j]
            right = block * misc[384:448] * inside[j]
            w_out[:, j * 256 : j * 256 + LANES] = left.astype(BF16)
            w_out[:, j * 256 + LANES : (j + 1) * 256] = right.astype(BF16)

    finish(weights.at[pl.ds(0, WIDTH - 1)], pack_recv)
    prepare(jnp.int32(0))

    near_places = [
        (distance, role(lax.rem(w + distance + WIDTH, WIDTH), s)) for distance in (2, -2, 1, -1)
    ]
    far_places = {displacement: around(displacement) for displacement in AROUND}

    def near(step):
        for distance, device in near_places:
            send(
                state.at[step, 2], state.at[step, 2 - distance],
                near_send.at[step], near_recv.at[step], device,
            )

    def far(step, displacements):
        for displacement in displacements:
            send(
                gathered.at[step, s], gathered.at[step, s],
                far_send.at[step],
                far_late.at[step] if displacement[0] == 2 else far_recv.at[step],
                far_places[displacement],
            )

    finish(partial_land.at[pl.ds(0, COILS - 1)], part_recv)
    total = partial_land[0]
    for n in range(1, COILS):
        total = total + partial_land[n]
    state[0, 2] = total[0:8]
    near(0)
    energy[...] = total[8:16]
    memory[...] = jnp.zeros_like(memory)
    sums[...] = jnp.zeros_like(sums)
    q_plain[...] = jnp.zeros_like(q_plain)
    q_masked[...] = jnp.zeros_like(q_masked)

    def normal(step):
        v = [[jnp.zeros((16, LANES), F32)] * 2 for _ in range(4)]
        for blocks, count, sem in (((0, 1, 2), 11, far_recv), ((3,), 4, far_late)):
            finish(gathered.at[step, pl.ds(0, count)], sem.at[step])
            for block in blocks:
                row = lax.rem(y + ROWS[block], 4)
                p = []
                for a in range(4):
                    res, ims = [], []
                    for inner in range(4):
                        other = row * 4 + inner
                        re = gathered[step, other, 2 * a : 2 * a + 1, :]
                        im = gathered[step, other, 2 * a + 1 : 2 * a + 2, :]
                        span = pl.ds(pl.multiple_of(other * 16, 16), 16)
                        map_re = maps_all[2 * a, span, :]
                        map_im = maps_all[2 * a + 1, span, :]
                        res.append(map_re * re - map_im * im)
                        ims.append(map_re * im + map_im * re)
                    p.append((jnp.concatenate(res, axis=0), jnp.concatenate(ims, axis=0)))
                residues = quarters_to_residues(p)
                for m in range(4):
                    spectrum[m, pl.ds(block * 64, 64), :] = triple(*residues[m])
            start, size = blocks[0] * 64, len(blocks) * 64
            for m in range(4):
                lines = product(spectrum[m, pl.ds(start, size), :], tf(m))
                re, im = v[m]
                for n in range(size // 16):
                    other = start // 16 + n
                    g_re = lattice[m, 0, other : other + 1, :]
                    g_im = lattice[m, 1, other : other + 1, :]
                    x_re = lines[n * 16 : (n + 1) * 16, :LANES]
                    x_im = lines[n * 16 : (n + 1) * 16, LANES:]
                    re = re + (g_re * x_re - g_im * x_im)
                    im = im + (g_re * x_im + g_im * x_re)
                v[m] = [re, im]
        back = inverse_lines(v, ti)
        rows = []
        mine = pl.ds(pl.multiple_of(s * 16, 16), 16)
        for a in range(4):
            map_re, map_im = maps_all[2 * a, mine, :], maps_all[2 * a + 1, mine, :]
            rows.append(jnp.sum(map_re * back[a][0] + map_im * back[a][1], axis=0, keepdims=True))
            rows.append(jnp.sum(map_re * back[a][1] - map_im * back[a][0], axis=0, keepdims=True))
        return jnp.concatenate(rows, axis=0)

    def arrived(step):
        finish(gathered.at[step, pl.ds(0, 11)], far_recv.at[step])
        finish(gathered.at[step, pl.ds(0, 4)], far_late.at[step])

    def accumulate(older):
        memory[...] = memory[...] * (1.0 - step_size(cascade_of(older))) + normal(older)

    def surroundings(step):
        finish(state.at[step, pl.ds(0, 4)], near_recv.at[step])
        taps = []
        for column in range(5):
            at_w = w + (column - 2)
            tile = state[step, column]
            if column != 2:
                tile = jnp.where((at_w >= 0) & (at_w < WIDTH), tile, jnp.zeros_like(tile))
            before, after = shifted(tile)
            taps += [before, tile, after]
        return jnp.concatenate(taps, axis=0)

    def enter(taps):
        high = taps.astype(BF16).astype(F32)
        low = taps - high
        rest = jnp.zeros((40, LANES), F32)
        columns = []
        for j in range(3):
            span = slice(24 * j, 24 * j + 72)
            columns.append(jnp.concatenate([high[span], low[span], high[span], rest], axis=0))
        return product(w_in[...], jnp.concatenate(columns, axis=1).astype(BF16))

    def leave(step, values):
        stack = jnp.concatenate([values[:, j * LANES : (j + 1) * LANES] for j in range(3)], axis=0)
        stack_high, stack_low = parts(stack)
        first = product(w_out[...], stack_high)
        second = product(w_out[0:32, :], stack_low)
        response = first[0:24] + first[32:56] + second[0:24]
        before, _ = shifted(response[0:8])
        _, after = shifted(response[16:24])
        gathered[step, s] = before + response[8:16] + after

    def activate(cascade, taps):
        before = enter(taps)
        gate = 1.0 / (1.0 + jnp.exp(-before))
        after = before * gate
        slope[cascade] = gate + after * (1.0 - gate)
        centre[cascade] = after[:, LANES : 2 * LANES]
        taps_saved[cascade] = taps[24:96]
        return after

    def advance(step):
        state[step + 1, 2] = (
            state[step, 2] - step_size(cascade_of(step)) * memory[...]
            + energy[...] * gathered[step, s]
        )
        near(step + 1)

    def forward(step, carry):
        leave(step, activate(step, surroundings(step)))

        @pl.when(step < CASC - 2)
        def _():
            far(step, AROUND[:LONG])

        @pl.when(step == 1)
        def _():
            finish(maps_land.at[pl.ds(0, COILS - 1)], maps_recv)
            for coil in range(COILS):
                block = padded(maps_land[coil]).T
                for plane in range(8):
                    maps_all[plane, pl.ds(coil, SLICES, stride=16), :] = block[
                        plane * SLICES : (plane + 1) * SLICES
                    ]

        @pl.when(step >= 1)
        def _():
            accumulate(step - 1)

        advance(step)

        @pl.when(step < CASC - 2)
        def _():
            far(step, AROUND[LONG:])

        @pl.when(step == 2)
        def _():
            finish(ending_land.at[pl.ds(0, COILS - 1)], end_recv)
            total = ending_land[0]
            for n in range(1, COILS):
                total = total + ending_land[n]
            state[CASC, 2] = total[0:8]
            near(CASC)
            final[...] = total[8:16]

        sums[step + 1] = sums[step] * (1.0 - step_size(step)) + gathered[step, s]
        prepare(step + 1)
        return carry

    lax.fori_loop(0, CASC - 1, forward, jnp.int32(0))
    activate(CASC - 1, surroundings(CASC - 1))
    prepare(jnp.int32(CASC))
    memory[...] = final[...]

    def filter_grads(cascade, taps):
        grads = []
        pairs = (
            (hidden[:, LANES : 2 * LANES], taps_saved[cascade]),
            (centre[cascade], taps),
        )
        for values, near_taps in pairs:
            left_high, left_low = parts(values)
            right = jnp.concatenate([near_taps, jnp.zeros((56, LANES), F32)], axis=0)
            right_high, right_low = parts(right)
            full = product_nt(
                jnp.concatenate([left_high, left_low, left_high], axis=1),
                jnp.concatenate([right_high, right_high, right_low], axis=1),
            ) * misc[64:320]
            grads.append(full[0:64] + full[64:128] + full[128:192] + full[192:256])
        fold = misc[16:64].astype(BF16)
        folded = product_nt(
            jnp.concatenate([fold, fold, fold], axis=1), three(jnp.concatenate(grads, axis=0))
        )
        lanes = lax.broadcasted_iota(jnp.int32, (24, LANES), 1)
        sizes = -jnp.sum(sums[cascade] * memory[...], axis=0, keepdims=True)
        w_send[cascade] = jnp.where(
            row24 == 18, sizes, jnp.where(lanes < 64, folded[0:24], folded[24:48])
        )

        @pl.when(g == cascade)
        def _():
            w_land[g] = w_send[cascade]

        @pl.when(g != cascade)
        def _():
            send(
                w_send.at[cascade], w_land.at[g], ws_send.at[cascade], ws_recv, place(cascade, k)
            )

    def collect(cascade):
        keep = 1.0 - step_size(cascade)
        slot = STEPS - 1 - cascade
        images = gathered[slot].reshape(SLICES * 8, LANES)
        q_plain[...] = q_plain[...] + images
        q_masked[...] = q_masked[...] * keep + images
        target = jnp.where((cascade == 1) & (x_lo == 0), 0, cascade)

        @pl.when(lax.rem(target, 2) == x_lo)
        def _():
            q_out[cascade, 0] = q_plain[...].T[:QUARTER]
            q_out[cascade, 1] = q_masked[...].T[:QUARTER]

            @pl.when(g == target)
            def _():
                q_land[z] = q_out[cascade]

            @pl.when(g != target)
            def _():
                send(q_out.at[cascade], q_land.at[z], q_send, q_recv, place(target, k))

    def backward(step, carry):
        cascade = STEPS - 1 - step
        taps = surroundings(step)
        values = enter(taps) * slope[cascade]
        hidden[...] = values
        leave(step, values)
        taps_saved[CASC] = taps[24:96]
        ending = step == STEPS - 1

        @pl.when(jnp.logical_not(ending))
        def _():
            far(step, AROUND[:LONG])

        @pl.when(ending)
        def _():
            @pl.when(z == 0)
            def _():
                tail_land[0] = gathered[step, s]

            @pl.when(z != 0)
            def _():
                send(
                    gathered.at[step, s], tail_land.at[z], tail_send, tail_recv, place(x_lo, k)
                )

        @pl.when((step > CASC) & (step < STEPS - 1))
        def _():
            accumulate(step - 1)

        @pl.when(step < STEPS - 1)
        def _():
            advance(step)

        @pl.when(jnp.logical_not(ending))
        def _():
            far(step, AROUND[LONG:])
            prepare(step + 1)

        filter_grads(cascade, taps_saved[CASC])

        @pl.when(step == STEPS - 1)
        def _():
            arrived(step - 1)

        @pl.when(step > CASC)
        def _():
            collect(cascade + 1)

        return carry

    lax.fori_loop(CASC, STEPS, backward, jnp.int32(0))

    even = [(dy, x_at) for dy in (2, 1, 3, 0) for x_at in (0, 2)]

    @pl.when(z == 0)
    def _():
        finish(tail_land.at[pl.ds(0, 3)], tail_recv)
        for dy, x_at in even:
            at_s = 4 * lax.rem(y + dy, 4) + x_at

            @pl.when(at_s == s)
            def _():
                late_land[core, s] = tail_land[...]

            @pl.when(at_s != s)
            def _():
                send(
                    tail_land, late_land.at[core, s], late_send, late_recv, role(core, at_s)
                )

    finish(w_land.at[pl.ds(0, WIDTH - 1)], ws_recv)
    total = w_land[0]
    for n in range(1, WIDTH):
        total = total + w_land[n]
    w_pair[core] = total
    send(w_pair.at[core], w_pair.at[core], wp_send, wp_recv, place(g, 2 * pair + 1 - core))

    def spread_out(count, image_of, into):
        p = []
        for a in range(4):
            columns = [
                [
                    turned_maps[2 * a + part, pl.ds(at_w, SLICES, stride=WIDTH), :]
                    for at_w in range(WIDTH)
                ]
                for part in range(2)
            ]
            map_re = jnp.concatenate(columns[0], axis=0)
            map_im = jnp.concatenate(columns[1], axis=0)
            res, ims = [], []
            for image in range(count):
                re = image_of(image, 2 * a)
                im = image_of(image, 2 * a + 1)
                res.append(map_re * re - map_im * im)
                ims.append(map_re * im + map_im * re)
            p.append((jnp.concatenate(res, axis=0), jnp.concatenate(ims, axis=0)))
        residues = quarters_to_residues(p)
        for m in range(4):
            lines = product_nt(tft[m], triple(*residues[m]))
            fields = []
            for image in range(count):
                span = slice(image * LANES, (image + 1) * LANES)
                field = product(
                    triple(lines[0:QUARTER, span], lines[LANES : LANES + QUARTER, span]), dz()
                )
                fields.append((field[:, :LANES], field[:, LANES:]))
            into(pl.ds(m, QUARTER, stride=4), fields)

    keep = jnp.ones((1, LANES), F32)
    for cascade in range(CASC):
        factor = 1.0 - step_size(cascade)
        keep = jnp.where(cascade >= g, keep * factor, keep)
    late_factor = jnp.where(g == 0, 1.0 - step_size(0), jnp.ones((1, LANES), F32))

    finish(w_pair.at[0], wp_recv)
    w_all[pair] = w_pair[0] + w_pair[1]
    for dy in (2, 1, 3, 0):
        for dx in (2, 0):
            if dy or dx:
                send(
                    w_all.at[pair], w_all.at[pair], wa_send, wa_recv, around((dy, dx))
                )

    partner = place(g, 2 * pair + 1 - core)
    finish(q_land.at[pl.ds(0, 3)], q_recv)
    for at_z in range(4):
        for image in range(2):
            q_open[core, at_z, image] = padded(q_land[at_z, image]).T
    send(q_open.at[core], q_open.at[core], pass_send.at[0], pass_recv.at[0], partner)
    finish(q_open.at[0], pass_recv.at[0])

    def early(image, plane):
        return jnp.concatenate(
            [
                q_open[n % 2, n // 2, image, pl.ds(plane, SLICES, stride=8), :]
                for n in range(WIDTH)
            ],
            axis=0,
        )

    def first_part(rows, fields):
        on = sampled[rows, :] > 0.5
        for part in range(2):
            seed = cotangent[part, rows, :]
            grad_k[part, rows, :] = jnp.where(
                on, keep * seed + late_factor * fields[1][part], seed + fields[0][part]
            )

    spread_out(2, early, first_part)

    @pl.when(g == 0)
    def _():
        finish(late_land.at[0, pl.ds(0, SLICES - 1)], late_recv)
        send(late_land.at[core], late_land.at[core], pass_send.at[1], pass_recv.at[1], partner)
        finish(late_land.at[0], pass_recv.at[1])

        def late(image, plane):
            return jnp.concatenate(
                [late_land[n % 2, :, n // 2, plane, :] for n in range(WIDTH)], axis=0
            )

        def second_part(rows, fields):
            for part in range(2):
                grad_k[part, rows, :] = grad_k[part, rows, :] + fields[0][part]

        spread_out(1, late, second_part)

    finish(w_all.at[pl.ds(0, 7)], wa_recv)
    total = w_all[0]
    for n in range(1, 8):
        total = total + w_all[n]
    for tap in range(18):
        grad_w[tap] = total[tap : tap + 1]
    grad_w[18] = jnp.broadcast_to(jnp.sum(total[18:19], axis=1, keepdims=True), (1, LANES))

    finish(weights.at[pl.ds(0, WIDTH - 1)], pack_send)
    finish(partial_land.at[pl.ds(0, COILS - 1)], part_send)
    finish(ending_land.at[pl.ds(0, COILS - 1)], end_send)
    finish(maps_land.at[pl.ds(0, COILS - 1)], maps_send)
    finish(w_pair.at[0], wp_send)
    finish(w_all.at[pl.ds(0, 7)], wa_send)
    finish(q_land.at[pl.ds(0, 3)], q_send)
    finish(q_open.at[0], pass_send.at[0])

    @pl.when(z != 0)
    def _():
        finish(tail_land.at[0], tail_send)

    @pl.when((z == 0) & (x_lo == 1))
    def _():
        finish(late_land.at[0, pl.ds(0, 8)], late_send)

    @pl.when(g == 0)
    def _():
        finish(late_land.at[0, pl.ds(0, 7)], late_send)
        finish(late_land.at[0], pass_send.at[1])

    def drain(step, carry):
        @pl.when((step < CASC - 2) | ((step >= CASC) & (step < STEPS - 1)))
        def _():
            finish(gathered.at[step, pl.ds(0, COILS - 1)], far_send.at[step])

        finish(state.at[step, pl.ds(0, 4)], near_send.at[step])

        @pl.when((step < CASC) & (step != g))
        def _():
            finish(w_send.at[lax.rem(step, CASC)], ws_send.at[lax.rem(step, CASC)])

        return carry

    lax.fori_loop(0, STEPS, drain, jnp.int32(0))


def shards(measured, maps, mask, first_filters, second_filters, step_sizes, cotangent):
    tables = [jnp.asarray(table) for table in constants()]
    dma = pltpu.SemaphoreType.DMA
    field = pltpu.VMEM((2, LINES, LANES), F32)
    scratch = [
        field, field, field,
        pltpu.VMEM((SLICES, LINES), jnp.int32),
        pltpu.VMEM((18, 1, HIDDEN), F32),
        pltpu.VMEM((18, 1, HIDDEN), F32),
    ]
    whole_tables = tables[:5]
    scratch += [pltpu.VMEM(table.shape, table.dtype) for table in whole_tables]
    scratch += [
        pltpu.VMEM((48, LANES), F32),
        pltpu.VMEM((32, LANES), F32),
        dma((13,)),
        pltpu.VMEM((LINES, LANES), F32),
        pltpu.VMEM((3, 2, LINES, LANES), F32),
        pltpu.VMEM((8, LANES, LANES), F32),
        pltpu.VMEM((2, QUARTER, LANES), F32),
        pltpu.VMEM((COILS, QUARTER, LANES), F32),
        pltpu.VMEM((8, SLICES * COILS, LANES), F32),
        pltpu.VMEM((4, 2, SLICES, LANES), F32),
        pltpu.VMEM((8, SLICES, LANES), F32),
        pltpu.VMEM((SLICES * 16, LANES), F32),
        pltpu.VMEM((COILS, 16, LANES), F32),
        pltpu.VMEM((SLICES * 16, LANES), F32),
        pltpu.VMEM((COILS, 16, LANES), F32),
        pltpu.VMEM((CASC, 24, LANES), F32),
        pltpu.VMEM((256, 256), BF16),
        pltpu.VMEM((64, 768), BF16),
        pltpu.VMEM((STEPS, 5, 8, LANES), F32),
        pltpu.VMEM((STEPS, SLICES, 8, LANES), F32),
        pltpu.VMEM((CASC, 256, 3 * LANES), F32),
        pltpu.VMEM((CASC, 256, LANES), F32),
        pltpu.VMEM((CASC + 1, 72, LANES), F32),
        pltpu.VMEM((256, 3 * LANES), F32),
        pltpu.VMEM((4, 256, 768), BF16),
        pltpu.VMEM((8, LANES), F32),
        pltpu.VMEM((8, LANES), F32),
        pltpu.VMEM((8, LANES), F32),
        pltpu.VMEM((CASC, 8, LANES), F32),
        pltpu.VMEM((SLICES * 8, LANES), F32),
        pltpu.VMEM((SLICES * 8, LANES), F32),
        pltpu.VMEM((CASC, 2, QUARTER, LANES), F32),
        pltpu.VMEM((4, 2, QUARTER, LANES), F32),
        pltpu.VMEM((2, 4, 2, SLICES * 8, LANES), F32),
        pltpu.VMEM((4, 8, LANES), F32),
        pltpu.VMEM((2, SLICES, 4, 8, LANES), F32),
        pltpu.VMEM((CASC, 24, LANES), F32),
        pltpu.VMEM((WIDTH, 24, LANES), F32),
        pltpu.VMEM((2, 24, LANES), F32),
        pltpu.VMEM((8, 24, LANES), F32),
        dma, dma, dma, dma, dma, dma, dma, dma,
        dma((STEPS,)), dma((STEPS,)), dma((STEPS,)), dma((STEPS,)), dma((STEPS,)),
        dma, dma, dma, dma, dma, dma, dma((2,)), dma((2,)),
        dma((CASC,)), dma, dma, dma, dma, dma,
    ]
    there = pl.BlockSpec(memory_space=pltpu.HBM)
    whole = pl.BlockSpec(memory_space=pltpu.VMEM)
    first = jnp.transpose(first_filters, (2, 0, 1))
    second = jnp.transpose(second_filters, (1, 0, 2))
    operands = [measured[0], maps[0], cotangent[0], mask, first, second]
    grad_k, grad_w = pl.pallas_call(
        kernel,
        out_shape=[
            jax.ShapeDtypeStruct((2, LINES, LANES), F32),
            jax.ShapeDtypeStruct((19, 1, LANES), F32),
        ],
        in_specs=[there] * 6 + [pl.BlockSpec(memory_space=pltpu.SMEM)] + [there] * len(tables),
        out_specs=[whole, whole],
        scratch_shapes=scratch,
        compiler_params=pltpu.CompilerParams(
            collective_id=0, has_side_effects=True, vmem_limit_bytes=58 * 1024 * 1024
        ),
        name="cascades",
    )(*operands, step_sizes, *tables)
    first = jnp.transpose(grad_w[:18, :, :64], (1, 2, 0))
    second = jnp.transpose(grad_w[:18, :, 64:], (1, 0, 2))
    return grad_k[None, None], first, second, grad_w[18, 0, :1]


def solution(mesh):
    in_specs = (
        P("coil", None, None, None),
        P("coil", None, None, None),
        P(),
        P("segment", None, None),
        P("segment", None, None),
        P("segment"),
        P("coil", None, None, None),
    )
    out_specs = (
        P("segment", "coil", None, None, None),
        P("segment", None, None),
        P("segment", None, None),
        P("segment"),
    )
    return jax.shard_map(shards, mesh=mesh, in_specs=in_specs, out_specs=out_specs, check_vma=False)
```

```python
import functools

import jax
import jax.numpy as jnp
import ml_dtypes
import numpy as np
from jax import lax
from jax.experimental import pallas as pl
from jax.experimental.pallas import tpu as pltpu
from jax.sharding import PartitionSpec as P

F32 = jnp.float32
BF16 = jnp.bfloat16
LINES = 320
QUARTER = 80
LANES = 128
WIDTH = 8
SLICES = 16
COILS = 16
CASC = 8
STEPS = 2 * CASC
HIDDEN = 64
MESH = pl.DeviceIdType.MESH
AROUND = sorted(
    [(dy, dx) for dy in range(4) for dx in range(4) if dy or dx],
    key=lambda d: -(min(d[0], 4 - d[0]) + min(d[1], 4 - d[1])),
)
LONG = 11
ROWS = (0, 1, 3, 2)


def stacked(table):
    high = table.astype(ml_dtypes.bfloat16)
    low = (table - high.astype(np.float64)).astype(ml_dtypes.bfloat16)
    return np.concatenate([high, high, low], axis=-2)


@functools.lru_cache(maxsize=None)
def constants():
    forward = np.zeros((4, 256, 256))
    inverse = np.zeros((4, 256, 256))
    v = np.arange(QUARTER)[:, None]
    b = np.arange(QUARTER)[None, :]
    re, im = slice(0, QUARTER), slice(LANES, LANES + QUARTER)
    for m in range(4):
        angle = 2 * np.pi * (((4 * v + m) * b) % LINES) / LINES
        cosine = np.cos(angle) / np.sqrt(LINES)
        sine = np.sin(angle) / np.sqrt(LINES)
        forward[m, re, re] = cosine.T
        forward[m, re, im] = -sine.T
        forward[m, im, re] = sine.T
        forward[m, im, im] = cosine.T
        inverse[m, re, re] = cosine
        inverse[m, re, im] = sine
        inverse[m, im, re] = -sine
        inverse[m, im, im] = cosine
    tf = stacked(forward)
    ti = stacked(inverse)
    tft = np.ascontiguousarray(np.swapaxes(tf, 1, 2))

    dz = np.zeros((256, 256))
    for w in range(WIDTH):
        for s in range(SLICES):
            for kz in range(SLICES):
                angle = 2 * np.pi * (s * kz % SLICES) / SLICES
                row, lane = w * SLICES + s, kz * WIDTH + w
                dz[row, lane] = np.cos(angle) / 4
                dz[row, LANES + lane] = -np.sin(angle) / 4
                dz[LANES + row, lane] = np.sin(angle) / 4
                dz[LANES + row, LANES + lane] = np.cos(angle) / 4
    dz = stacked(dz)

    rep = np.zeros((SLICES, LANES), np.float32)
    for kz in range(SLICES):
        rep[kz, kz * WIDTH : (kz + 1) * WIDTH] = 1
    outward = np.zeros((16, 48, LANES), np.float32)
    for g in range(WIDTH):
        for x_hi in range(2):
            for q in range(16):
                j = q % 8
                s = 2 * j + (g % 2 if j % 2 == x_hi else 1 - g % 2)
                w = 2 * (g // 2) + q // 8
                outward[2 * g + x_hi, 32 + q, s * WIDTH + w] = 1
                for kz in range(SLICES):
                    angle = 2 * np.pi * (s * kz % SLICES) / SLICES
                    outward[2 * g + x_hi, q, kz * WIDTH + w] = np.cos(angle) / 4
                    outward[2 * g + x_hi, 16 + q, kz * WIDTH + w] = np.sin(angle) / 4
    gc = np.zeros((SLICES, 32, LANES), np.float32)
    for kz in range(SLICES):
        for s in range(SLICES):
            for n in range(SLICES):
                other = 4 * ((s // 4 + ROWS[n // 4]) % 4) + n % 4
                angle = 2 * np.pi * ((s - other) * kz % SLICES) / SLICES
                gc[s, n, kz * WIDTH] = np.cos(angle) / 16
                gc[s, 16 + n, kz * WIDTH] = np.sin(angle) / 16

    expand = np.zeros((2, LANES, 4 * 256), np.float32)
    choose = np.zeros((2, 3 * 64, LANES), np.float32)
    fold = np.zeros((2, 24, LANES), np.float32)
    amask = np.zeros((64, 256), np.float32)
    gmask = np.zeros((256, LANES), np.float32)
    for ch in range(2):
        for dh in range(3):
            for dw in range(3):
                taps = (ch * 9 + dh * 3 + dw, ch * 9 + (2 - dh) * 3 + (2 - dw))
                for way in range(2):
                    for a in range(4):
                        lane = dw * 24 + dh * 8 + a * 2 + ch
                        expand[way, taps[way], a * 256 + lane] = 1
                        expand[way, taps[way], a * 256 + 72 + lane] = 1
                        expand[way, 24 + taps[way], a * 256 + 144 + lane] = 1
                        fold[way, taps[way], lane] = 1
                        for hl in range(2):
                            row = hl * 32 + dh * 8 + a * 2 + ch
                            choose[way, dw * 64 + row, hl * 24 + taps[way]] = 1
                            amask[row, a * 64 : (a + 1) * 64] = 1
                        gmask[a * 64 : (a + 1) * 64, lane] = 1
    bf = ml_dtypes.bfloat16
    wide = np.concatenate([tf.reshape(-1, 256), ti.reshape(-1, 256), dz], axis=0)
    misc = np.concatenate(
        [rep, fold.reshape(48, LANES), gmask, amask[:, :LANES], amask[:, LANES:]], axis=0
    )
    return wide, tft, expand.astype(bf), choose.astype(bf), misc, outward, gc


def product(left, right):
    return jnp.dot(left, right, preferred_element_type=F32)


def product_nt(left, right):
    return lax.dot_general(left, right, (((1,), (1,)), ((), ())), preferred_element_type=F32)


def parts(values):
    high = values.astype(BF16)
    low = (values - high.astype(F32)).astype(BF16)
    return high, low


def three(values):
    first = values.astype(BF16)
    rest = values - first.astype(F32)
    second = rest.astype(BF16)
    third = (rest - second.astype(F32)).astype(BF16)
    return jnp.concatenate([first, second, third], axis=1)


def triple(re, im):
    re_high, re_low = parts(re)
    im_high, im_low = parts(im)
    return jnp.concatenate([re_high, im_high, re_low, im_low, re_high, im_high], axis=1)


def shifted(tile):
    lane = lax.broadcasted_iota(jnp.int32, (8, LANES), 1)
    row = lax.broadcasted_iota(jnp.int32, (8, LANES), 0)
    zero = jnp.zeros_like(tile)
    last = QUARTER - 1
    next_first = pltpu.roll(pltpu.roll(tile, last, 1), 6, 0)
    after = jnp.where(
        lane < last,
        pltpu.roll(tile, LANES - 1, 1),
        jnp.where((lane == last) & (row < 6), next_first, zero),
    )
    previous_last = pltpu.roll(pltpu.roll(tile, LANES - last, 1), 2, 0)
    before = jnp.where(
        (lane >= 1) & (lane < QUARTER),
        pltpu.roll(tile, 1, 1),
        jnp.where((lane == 0) & (row >= 2), previous_last, zero),
    )
    return before, after


def quarters_to_residues(p):
    t0 = [p[0][k] + p[2][k] for k in range(2)]
    t1 = [p[0][k] - p[2][k] for k in range(2)]
    t2 = [p[1][k] + p[3][k] for k in range(2)]
    t3 = [p[1][k] - p[3][k] for k in range(2)]
    return (
        (t0[0] + t2[0], t0[1] + t2[1]),
        (t1[0] + t3[1], t1[1] - t3[0]),
        (t0[0] - t2[0], t0[1] - t2[1]),
        (t1[0] - t3[1], t1[1] + t3[0]),
    )


def residues_to_quarters(z):
    t0 = [z[0][k] + z[2][k] for k in range(2)]
    t1 = [z[0][k] - z[2][k] for k in range(2)]
    t2 = [z[1][k] + z[3][k] for k in range(2)]
    t3 = [z[1][k] - z[3][k] for k in range(2)]
    return (
        (t0[0] + t2[0], t0[1] + t2[1]),
        (t1[0] - t3[1], t1[1] + t3[0]),
        (t0[0] - t2[0], t0[1] - t2[1]),
        (t1[0] + t3[1], t1[1] - t3[0]),
    )


def inverse_lines(v, table):
    z = []
    for m in range(4):
        result = product(triple(*v[m]), table(m))
        z.append((result[:, :LANES], result[:, LANES:]))
    return residues_to_quarters(z)


def kernel(
    measured_hbm, maps_hbm, cotangent_hbm, mask_hbm, first_hbm, second_hbm, size_ref,
    wide_hbm, tft_hbm, expand_hbm, choose_hbm, misc_hbm, outward_hbm, gc_hbm,
    grad_k, grad_w,
    measured, maps, cotangent, mask, first_in, second_in,
    wide, tft, expand, choose, misc, outward, gc, load_sem,
    sampled, masked, turned_maps, maps_out, maps_land, maps_all, lattice, picked, partial_out, partial_land,
    ending_out, ending_land,
    weights, w_in, w_out, state, gathered, slope, centre, taps_saved, hidden, spectrum,
    energy, memory, final, sums, q_plain, q_masked, q_out, q_land, q_open, tail_land, late_land,
    w_send, w_land, w_pair, w_all,
    pack_send, pack_recv, part_send, part_recv, end_send, end_recv, maps_send, maps_recv,
    near_send, near_recv, far_send, far_recv, far_late, q_send, q_recv,
    tail_send, tail_recv, late_send, late_recv, pass_send, pass_recv,
    ws_send, ws_recv, wp_send, wp_recv, wa_send, wa_recv,
):
    g = lax.axis_index("segment")
    k = lax.axis_index("coil")
    z, x_lo = lax.div(g, 2), lax.rem(g, 2)
    pair, core = lax.div(k, 2), lax.rem(k, 2)
    y, x_hi = lax.div(pair, 2), lax.rem(pair, 2)
    w = 2 * z + core
    s = 2 * pair + x_lo
    x = 2 * x_hi + x_lo

    def role(at_w, at_s):
        return {
            "segment": 2 * lax.div(at_w, 2) + lax.rem(at_s, 2),
            "coil": 2 * lax.div(at_s, 2) + lax.rem(at_w, 2),
        }

    def around(displacement):
        dy, dx = displacement
        return role(w, 4 * lax.rem(y + dy, 4) + lax.rem(x + dx, 4))

    def place(at_g, at_k):
        return {"segment": at_g, "coil": at_k}

    receivers = []
    for dy in (2, 1, 3, 0):
        for flip in range(2):
            for at_core in range(2):
                if dy or flip:
                    at_k = 4 * lax.rem(y + dy, 4) + 2 * lax.rem(x_hi + flip, 2) + at_core
                    at_g = g if flip == 0 else 2 * z + 1 - x_lo
                    receivers.append((at_g, at_k, at_core))
    receivers.append((g, 2 * pair + 1 - core, 1 - core))
    segment_peers = [lax.rem(g + n, WIDTH) for n in range(1, WIDTH)]

    def send(source, target, send_sem, recv_sem, device):
        pltpu.make_async_remote_copy(
            src_ref=source, dst_ref=target, send_sem=send_sem, recv_sem=recv_sem,
            device_id=device, device_id_type=MESH,
        ).start()

    def finish(extent, sem):
        pltpu.make_async_copy(extent, extent, sem).wait()

    loads = (
        (maps_hbm, maps), (measured_hbm, measured), (mask_hbm, mask), (misc_hbm, misc),
        (outward_hbm.at[2 * g + x_hi], outward), (wide_hbm, wide),
        (first_hbm, first_in), (second_hbm, second_in), (cotangent_hbm, cotangent),
        (gc_hbm.at[s], gc), (expand_hbm, expand), (choose_hbm, choose), (tft_hbm, tft),
    )
    loads = [
        pltpu.make_async_copy(source, target, load_sem.at[n])
        for n, (source, target) in enumerate(loads)
    ]
    for load in loads[:6]:
        load.start()

    barrier = pltpu.get_barrier_semaphore()

    def greet(device):
        pl.semaphore_signal(barrier, inc=1, device_id=device, device_id_type=MESH)

    for dy, dx in AROUND:
        if dx:
            other = lax.rem(x + dx, 4)

            @pl.when(other != 3 - x)
            def _():
                greet(role(w, 4 * lax.rem(y + dy, 4) + other))

    for turn in (2, 1, 3):
        at_z = lax.rem(z + turn, 4)
        greet(place(2 * at_z + 1 - x_lo, k))
        for at_core in range(2):
            greet(place(2 * at_z + x_lo, 2 * pair + at_core))
    for at_g, at_k, _ in receivers:
        greet(place(at_g, at_k))
    for load in loads[6:]:
        load.start()

    def tf(m):
        return wide[m * 768 : (m + 1) * 768, :]

    def ti(m):
        return wide[3072 + m * 768 : 3072 + (m + 1) * 768, :]

    def dz():
        return wide[6144:6912, :]

    blank = jnp.zeros((LANES - QUARTER, LANES), F32)

    def padded(values):
        return jnp.concatenate([values, blank], axis=0)

    loads[0].wait()
    for part in range(2):
        for a in range(4):
            block = padded(maps[part, a * QUARTER : (a + 1) * QUARTER, :])
            turned_maps[2 * a + part] = block.T
    for at_core in range(2):
        lines = [
            turned_maps[plane, pl.ds(2 * z + at_core, SLICES, stride=WIDTH), :]
            for plane in range(8)
        ]
        maps_out[at_core] = jnp.concatenate(lines, axis=0).T[:QUARTER]
    maps_land[k] = maps_out[core]

    for load in loads[1:5]:
        load.wait()
    sampled[...] = lax.dot_general(
        mask[...].astype(F32), misc[0:16], (((0,), (0,)), ((), ())), preferred_element_type=F32
    )
    spots = sampled[...]
    for part in range(2):
        masked[0, part] = measured[part] * spots
    c_high, c_low = parts(outward[0:32, :])
    c_left = jnp.concatenate([c_high, c_high, c_low], axis=1)

    def to_images(fields):
        spectra = []
        for m in range(4):
            rows = pl.ds(m, QUARTER, stride=4)
            blocks = [padded(masked[field, part, rows, :]) for field in fields for part in range(2)]
            high, low = parts(jnp.concatenate(blocks, axis=0))
            both = product_nt(c_left, jnp.concatenate([high, low, high], axis=1))
            res, ims = [], []
            for n in range(len(fields)):
                from_re = both[:, n * 256 : n * 256 + LANES]
                from_im = both[:, n * 256 + LANES : n * 256 + 256]
                res.append(from_re[:16] - from_im[16:])
                ims.append(from_im[:16] + from_re[16:])
            spectra.append((jnp.concatenate(res, axis=0), jnp.concatenate(ims, axis=0)))
        return inverse_lines(spectra, ti)

    def weigh(images, count, out):
        for a in range(4):
            map_re, map_im = picked[2 * a], picked[2 * a + 1]
            for n in range(count):
                re = images[a][0][n * 16 : (n + 1) * 16]
                im = images[a][1][n * 16 : (n + 1) * 16]
                row = n * 8 + 2 * a
                out[pl.ds(row, 16, stride=16), :] = map_re * re + map_im * im
                out[pl.ds(row + 1, 16, stride=16), :] = map_re * im - map_im * re

    pick = outward[32:48, :].astype(BF16)
    for plane in range(8):
        split = three(turned_maps[plane])
        picked[plane] = (
            product(pick, split[:, :LANES])
            + product(pick, split[:, LANES : 2 * LANES])
            + product(pick, split[:, 2 * LANES :])
        )
    for a in range(4):
        power = picked[2 * a] * picked[2 * a] + picked[2 * a + 1] * picked[2 * a + 1]
        partial_out[pl.ds(8 + 2 * a, 16, stride=16), :] = power
        partial_out[pl.ds(9 + 2 * a, 16, stride=16), :] = power
    loads[5].wait()
    weigh(to_images((0,)), 1, partial_out)

    for load in loads[6:8]:
        load.wait()
    hidden[0:64, 0:LANES] = jnp.zeros((64, LANES), F32)
    for tap in range(18):
        hidden[tap : tap + 1, 0:64] = first_in[tap]
        hidden[32 + tap : 33 + tap, 0:64] = second_in[tap]
    row24 = lax.broadcasted_iota(jnp.int32, (24, LANES), 0)
    weights[g] = jnp.where(
        row24 < 18,
        hidden[0:24, 0:LANES] + pltpu.roll(hidden[32:56, 0:LANES], 64, 1),
        jnp.full((24, LANES), size_ref[0], F32),
    )

    pl.semaphore_wait(barrier, 32)

    def block_of(at_k):
        q = lax.rem(at_k, 2) * 8 + lax.div(at_k, 2)
        return pl.ds(pl.multiple_of(q * 16, 16), 16)

    for at_g, at_k, _ in receivers:
        send(
            partial_out.at[block_of(at_k)], partial_land.at[k], part_send, part_recv,
            place(at_g, at_k),
        )
    partial_land[k] = partial_out[block_of(k), :]
    for at_g in segment_peers:
        send(weights.at[g], weights.at[g], pack_send, pack_recv, place(at_g, k))
    for at_g, at_k, at_core in receivers:
        send(maps_out.at[at_core], maps_land.at[k], maps_send, maps_recv, place(at_g, at_k))

    loads[8].wait()
    for part in range(2):
        masked[1, part] = cotangent[part]
        masked[2, part] = cotangent[part] * sampled[...]
    weigh(to_images((1, 2)), 2, ending_out)
    for at_g, at_k, _ in receivers:
        send(
            ending_out.at[block_of(at_k)], ending_land.at[k], end_send, end_recv,
            place(at_g, at_k),
        )
    ending_land[k] = ending_out[block_of(k), :]

    for load in loads[9:]:
        load.wait()
    g_high, g_low = parts(gc[...])
    g_left = jnp.concatenate([g_high, g_low], axis=1)
    for m in range(4):
        spots_m = padded(sampled[pl.ds(m, QUARTER, stride=4), :]).astype(BF16)
        rows = product_nt(g_left, jnp.concatenate([spots_m, spots_m], axis=1))
        lattice[m, 0] = rows[:16]
        lattice[m, 1] = rows[16:]

    def cascade_of(step):
        return jnp.where(step < CASC, step, STEPS - 1 - step)

    def step_size(cascade):
        return weights[cascade, 18:19, :]

    def prepare(step):
        way = (step >= CASC).astype(jnp.int32)
        raw = weights[cascade_of(step)]
        lane = lax.broadcasted_iota(jnp.int32, raw.shape, 1)
        turned = pltpu.roll(raw, 64, 1)
        first = jnp.where(lane < 64, raw, turned)
        second = jnp.where(lane < 64, turned, raw)
        enter = jnp.where(way == 0, first, second)
        leave = jnp.where(way == 0, second, first)

        def columns(values):
            high = values.astype(BF16).astype(F32)
            return jnp.concatenate([high, values - high, jnp.zeros((80, LANES), F32)], axis=0)

        flat = columns(enter).T[:64].astype(BF16)
        spread = product(flat, expand[way]).astype(BF16)
        for a in range(4):
            w_in[a * 64 : (a + 1) * 64, :] = spread[:, a * 256 : (a + 1) * 256]
        tall = product(choose[way], columns(leave).astype(BF16))
        inside = (
            jnp.where(w > 0, 1.0, 0.0), jnp.float32(1.0), jnp.where(w < WIDTH - 1, 1.0, 0.0)
        )
        for j in range(3):
            block = tall[j * 64 : (j + 1) * 64]
            left = block * misc[320:384] * inside[j]
            right = block * misc[384:448] * inside[j]
            w_out[:, j * 256 : j * 256 + LANES] = left.astype(BF16)
            w_out[:, j * 256 + LANES : (j + 1) * 256] = right.astype(BF16)

    finish(weights.at[pl.ds(0, WIDTH - 1)], pack_recv)
    prepare(jnp.int32(0))

    def near(step):
        for distance in (2, -2, 1, -1):
            send(
                state.at[step, 2], state.at[step, 2 - distance],
                near_send.at[step], near_recv.at[step],
                role(lax.rem(w + distance + WIDTH, WIDTH), s),
            )

    def far(step, displacements):
        for displacement in displacements:
            send(
                gathered.at[step, s], gathered.at[step, s],
                far_send.at[step],
                far_late.at[step] if displacement[0] == 2 else far_recv.at[step],
                around(displacement),
            )

    finish(partial_land.at[pl.ds(0, COILS - 1)], part_recv)
    total = partial_land[0]
    for n in range(1, COILS):
        total = total + partial_land[n]
    state[0, 2] = total[0:8]
    near(0)
    energy[...] = total[8:16]
    memory[...] = jnp.zeros_like(memory)
    sums[...] = jnp.zeros_like(sums)
    q_plain[...] = jnp.zeros_like(q_plain)
    q_masked[...] = jnp.zeros_like(q_masked)

    def normal(step):
        v = [[jnp.zeros((16, LANES), F32)] * 2 for _ in range(4)]
        for blocks, count, sem in (((0, 1, 2), 11, far_recv), ((3,), 4, far_late)):
            finish(gathered.at[step, pl.ds(0, count)], sem.at[step])
            for block in blocks:
                row = lax.rem(y + ROWS[block], 4)
                p = []
                for a in range(4):
                    res, ims = [], []
                    for inner in range(4):
                        other = row * 4 + inner
                        re = gathered[step, other, 2 * a : 2 * a + 1, :]
                        im = gathered[step, other, 2 * a + 1 : 2 * a + 2, :]
                        span = pl.ds(pl.multiple_of(other * 16, 16), 16)
                        map_re = maps_all[2 * a, span, :]
                        map_im = maps_all[2 * a + 1, span, :]
                        res.append(map_re * re - map_im * im)
                        ims.append(map_re * im + map_im * re)
                    p.append((jnp.concatenate(res, axis=0), jnp.concatenate(ims, axis=0)))
                residues = quarters_to_residues(p)
                for m in range(4):
                    spectrum[m, pl.ds(block * 64, 64), :] = triple(*residues[m])
            start, size = blocks[0] * 64, len(blocks) * 64
            for m in range(4):
                lines = product(spectrum[m, pl.ds(start, size), :], tf(m))
                re, im = v[m]
                for n in range(size // 16):
                    other = start // 16 + n
                    g_re = lattice[m, 0, other : other + 1, :]
                    g_im = lattice[m, 1, other : other + 1, :]
                    x_re = lines[n * 16 : (n + 1) * 16, :LANES]
                    x_im = lines[n * 16 : (n + 1) * 16, LANES:]
                    re = re + (g_re * x_re - g_im * x_im)
                    im = im + (g_re * x_im + g_im * x_re)
                v[m] = [re, im]
        back = inverse_lines(v, ti)
        rows = []
        mine = pl.ds(pl.multiple_of(s * 16, 16), 16)
        for a in range(4):
            map_re, map_im = maps_all[2 * a, mine, :], maps_all[2 * a + 1, mine, :]
            rows.append(jnp.sum(map_re * back[a][0] + map_im * back[a][1], axis=0, keepdims=True))
            rows.append(jnp.sum(map_re * back[a][1] - map_im * back[a][0], axis=0, keepdims=True))
        return jnp.concatenate(rows, axis=0)

    def arrived(step):
        finish(gathered.at[step, pl.ds(0, 11)], far_recv.at[step])
        finish(gathered.at[step, pl.ds(0, 4)], far_late.at[step])

    def accumulate(older):
        memory[...] = memory[...] * (1.0 - step_size(cascade_of(older))) + normal(older)

    def surroundings(step):
        finish(state.at[step, pl.ds(0, 4)], near_recv.at[step])
        taps = []
        for column in range(5):
            at_w = w + (column - 2)
            tile = state[step, column]
            if column != 2:
                tile = jnp.where((at_w >= 0) & (at_w < WIDTH), tile, jnp.zeros_like(tile))
            before, after = shifted(tile)
            taps += [before, tile, after]
        return jnp.concatenate(taps, axis=0)

    def enter(taps):
        high = taps.astype(BF16).astype(F32)
        low = taps - high
        rest = jnp.zeros((40, LANES), F32)
        columns = []
        for j in range(3):
            span = slice(24 * j, 24 * j + 72)
            columns.append(jnp.concatenate([high[span], low[span], high[span], rest], axis=0))
        return product(w_in[...], jnp.concatenate(columns, axis=1).astype(BF16))

    def leave(step, values):
        stack = jnp.concatenate([values[:, j * LANES : (j + 1) * LANES] for j in range(3)], axis=0)
        stack_high, stack_low = parts(stack)
        first = product(w_out[...], stack_high)
        second = product(w_out[0:32, :], stack_low)
        response = first[0:24] + first[32:56] + second[0:24]
        before, _ = shifted(response[0:8])
        _, after = shifted(response[16:24])
        gathered[step, s] = before + response[8:16] + after

    def activate(cascade, taps):
        before = enter(taps)
        gate = 1.0 / (1.0 + jnp.exp(-before))
        after = before * gate
        slope[cascade] = gate + after * (1.0 - gate)
        centre[cascade] = after[:, LANES : 2 * LANES]
        taps_saved[cascade] = taps[24:96]
        return after

    def advance(step):
        state[step + 1, 2] = (
            state[step, 2] - step_size(cascade_of(step)) * memory[...]
            + energy[...] * gathered[step, s]
        )
        near(step + 1)

    def forward(step, carry):
        leave(step, activate(step, surroundings(step)))

        @pl.when(step < CASC - 2)
        def _():
            far(step, AROUND[:LONG])

        @pl.when(step >= 1)
        def _():
            accumulate(step - 1)

        advance(step)

        @pl.when(step < CASC - 2)
        def _():
            far(step, AROUND[LONG:])

        @pl.when(step == 2)
        def _():
            finish(ending_land.at[pl.ds(0, COILS - 1)], end_recv)
            total = ending_land[0]
            for n in range(1, COILS):
                total = total + ending_land[n]
            state[CASC, 2] = total[0:8]
            near(CASC)
            final[...] = total[8:16]

        sums[step + 1] = sums[step] * (1.0 - step_size(step)) + gathered[step, s]
        prepare(step + 1)

        @pl.when(step == 0)
        def _():
            finish(maps_land.at[pl.ds(0, COILS - 1)], maps_recv)
            for coil in range(COILS):
                block = padded(maps_land[coil]).T
                for plane in range(8):
                    maps_all[plane, pl.ds(coil, SLICES, stride=16), :] = block[
                        plane * SLICES : (plane + 1) * SLICES
                    ]

        return carry

    lax.fori_loop(0, CASC - 1, forward, jnp.int32(0))
    activate(CASC - 1, surroundings(CASC - 1))
    prepare(jnp.int32(CASC))
    memory[...] = final[...]

    def filter_grads(cascade, taps):
        grads = []
        pairs = (
            (hidden[:, LANES : 2 * LANES], taps_saved[cascade]),
            (centre[cascade], taps),
        )
        for values, near_taps in pairs:
            left_high, left_low = parts(values)
            right = jnp.concatenate([near_taps, jnp.zeros((56, LANES), F32)], axis=0)
            right_high, right_low = parts(right)
            full = product_nt(
                jnp.concatenate([left_high, left_low, left_high], axis=1),
                jnp.concatenate([right_high, right_high, right_low], axis=1),
            ) * misc[64:320]
            grads.append(full[0:64] + full[64:128] + full[128:192] + full[192:256])
        fold = misc[16:64].astype(BF16)
        folded = product_nt(
            jnp.concatenate([fold, fold, fold], axis=1), three(jnp.concatenate(grads, axis=0))
        )
        lanes = lax.broadcasted_iota(jnp.int32, (24, LANES), 1)
        sizes = -jnp.sum(sums[cascade] * memory[...], axis=0, keepdims=True)
        w_send[cascade] = jnp.where(
            row24 == 18, sizes, jnp.where(lanes < 64, folded[0:24], folded[24:48])
        )

        @pl.when(g == cascade)
        def _():
            w_land[g] = w_send[cascade]

        @pl.when(g != cascade)
        def _():
            send(
                w_send.at[cascade], w_land.at[g], ws_send.at[cascade], ws_recv, place(cascade, k)
            )

    def collect(cascade):
        keep = 1.0 - step_size(cascade)
        slot = STEPS - 1 - cascade
        images = gathered[slot].reshape(SLICES * 8, LANES)
        q_plain[...] = q_plain[...] + images
        q_masked[...] = q_masked[...] * keep + images
        target = jnp.where((cascade == 1) & (x_lo == 0), 0, cascade)

        @pl.when(lax.rem(target, 2) == x_lo)
        def _():
            q_out[cascade, 0] = q_plain[...].T[:QUARTER]
            q_out[cascade, 1] = q_masked[...].T[:QUARTER]

            @pl.when(g == target)
            def _():
                q_land[z] = q_out[cascade]

            @pl.when(g != target)
            def _():
                send(q_out.at[cascade], q_land.at[z], q_send, q_recv, place(target, k))

    def backward(step, carry):
        cascade = STEPS - 1 - step
        taps = surroundings(step)
        values = enter(taps) * slope[cascade]
        hidden[...] = values
        leave(step, values)
        taps_saved[CASC] = taps[24:96]
        ending = step == STEPS - 1

        @pl.when(jnp.logical_not(ending))
        def _():
            far(step, AROUND[:LONG])

        @pl.when(ending)
        def _():
            @pl.when(z == 0)
            def _():
                tail_land[0] = gathered[step, s]

            @pl.when(z != 0)
            def _():
                send(
                    gathered.at[step, s], tail_land.at[z], tail_send, tail_recv, place(x_lo, k)
                )

        @pl.when((step > CASC) & (step < STEPS - 1))
        def _():
            accumulate(step - 1)

        @pl.when(step < STEPS - 1)
        def _():
            advance(step)

        @pl.when(jnp.logical_not(ending))
        def _():
            far(step, AROUND[LONG:])
            prepare(step + 1)

        filter_grads(cascade, taps_saved[CASC])

        @pl.when(step == STEPS - 1)
        def _():
            arrived(step - 1)

        @pl.when(step > CASC)
        def _():
            collect(cascade + 1)

        return carry

    lax.fori_loop(CASC, STEPS, backward, jnp.int32(0))

    even = [(dy, x_at) for dy in (2, 1, 3, 0) for x_at in (0, 2)]

    @pl.when(z == 0)
    def _():
        finish(tail_land.at[pl.ds(0, 3)], tail_recv)
        for dy, x_at in even:
            at_s = 4 * lax.rem(y + dy, 4) + x_at

            @pl.when(at_s == s)
            def _():
                late_land[core, s] = tail_land[...]

            @pl.when(at_s != s)
            def _():
                send(
                    tail_land, late_land.at[core, s], late_send, late_recv, role(core, at_s)
                )

    finish(w_land.at[pl.ds(0, WIDTH - 1)], ws_recv)
    total = w_land[0]
    for n in range(1, WIDTH):
        total = total + w_land[n]
    w_pair[core] = total
    send(w_pair.at[core], w_pair.at[core], wp_send, wp_recv, place(g, 2 * pair + 1 - core))

    def spread_out(count, image_of, into):
        p = []
        for a in range(4):
            columns = [
                [
                    turned_maps[2 * a + part, pl.ds(at_w, SLICES, stride=WIDTH), :]
                    for at_w in range(WIDTH)
                ]
                for part in range(2)
            ]
            map_re = jnp.concatenate(columns[0], axis=0)
            map_im = jnp.concatenate(columns[1], axis=0)
            res, ims = [], []
            for image in range(count):
                re = image_of(image, 2 * a)
                im = image_of(image, 2 * a + 1)
                res.append(map_re * re - map_im * im)
                ims.append(map_re * im + map_im * re)
            p.append((jnp.concatenate(res, axis=0), jnp.concatenate(ims, axis=0)))
        residues = quarters_to_residues(p)
        for m in range(4):
            lines = product_nt(tft[m], triple(*residues[m]))
            fields = []
            for image in range(count):
                span = slice(image * LANES, (image + 1) * LANES)
                field = product(
                    triple(lines[0:QUARTER, span], lines[LANES : LANES + QUARTER, span]), dz()
                )
                fields.append((field[:, :LANES], field[:, LANES:]))
            into(pl.ds(m, QUARTER, stride=4), fields)

    keep = jnp.ones((1, LANES), F32)
    for cascade in range(CASC):
        factor = 1.0 - step_size(cascade)
        keep = jnp.where(cascade >= g, keep * factor, keep)
    late_factor = jnp.where(g == 0, 1.0 - step_size(0), jnp.ones((1, LANES), F32))

    finish(w_pair.at[0], wp_recv)
    w_all[pair] = w_pair[0] + w_pair[1]
    for dy in (2, 1, 3, 0):
        for dx in (2, 0):
            if dy or dx:
                send(
                    w_all.at[pair], w_all.at[pair], wa_send, wa_recv, around((dy, dx))
                )

    partner = place(g, 2 * pair + 1 - core)
    finish(q_land.at[pl.ds(0, 3)], q_recv)
    for at_z in range(4):
        for image in range(2):
            q_open[core, at_z, image] = padded(q_land[at_z, image]).T
    send(q_open.at[core], q_open.at[core], pass_send.at[0], pass_recv.at[0], partner)
    finish(q_open.at[0], pass_recv.at[0])

    def early(image, plane):
        return jnp.concatenate(
            [
                q_open[n % 2, n // 2, image, pl.ds(plane, SLICES, stride=8), :]
                for n in range(WIDTH)
            ],
            axis=0,
        )

    def first_part(rows, fields):
        on = sampled[rows, :] > 0.5
        for part in range(2):
            seed = cotangent[part, rows, :]
            grad_k[part, rows, :] = jnp.where(
                on, keep * seed + late_factor * fields[1][part], seed + fields[0][part]
            )

    spread_out(2, early, first_part)

    @pl.when(g == 0)
    def _():
        finish(late_land.at[0, pl.ds(0, SLICES - 1)], late_recv)
        send(late_land.at[core], late_land.at[core], pass_send.at[1], pass_recv.at[1], partner)
        finish(late_land.at[0], pass_recv.at[1])

        def late(image, plane):
            return jnp.concatenate(
                [late_land[n % 2, :, n // 2, plane, :] for n in range(WIDTH)], axis=0
            )

        def second_part(rows, fields):
            for part in range(2):
                grad_k[part, rows, :] = grad_k[part, rows, :] + fields[0][part]

        spread_out(1, late, second_part)

    finish(w_all.at[pl.ds(0, 7)], wa_recv)
    total = w_all[0]
    for n in range(1, 8):
        total = total + w_all[n]
    for tap in range(18):
        grad_w[tap] = total[tap : tap + 1]
    grad_w[18] = jnp.broadcast_to(jnp.sum(total[18:19], axis=1, keepdims=True), (1, LANES))

    finish(weights.at[pl.ds(0, WIDTH - 1)], pack_send)
    finish(partial_land.at[pl.ds(0, COILS - 1)], part_send)
    finish(ending_land.at[pl.ds(0, COILS - 1)], end_send)
    finish(maps_land.at[pl.ds(0, COILS - 1)], maps_send)
    finish(w_pair.at[0], wp_send)
    finish(w_all.at[pl.ds(0, 7)], wa_send)
    finish(q_land.at[pl.ds(0, 3)], q_send)
    finish(q_open.at[0], pass_send.at[0])

    @pl.when(z != 0)
    def _():
        finish(tail_land.at[0], tail_send)

    @pl.when((z == 0) & (x_lo == 1))
    def _():
        finish(late_land.at[0, pl.ds(0, 8)], late_send)

    @pl.when(g == 0)
    def _():
        finish(late_land.at[0, pl.ds(0, 7)], late_send)
        finish(late_land.at[0], pass_send.at[1])

    def drain(step, carry):
        @pl.when((step < CASC - 2) | ((step >= CASC) & (step < STEPS - 1)))
        def _():
            finish(gathered.at[step, pl.ds(0, COILS - 1)], far_send.at[step])

        finish(state.at[step, pl.ds(0, 4)], near_send.at[step])

        @pl.when((step < CASC) & (step != g))
        def _():
            finish(w_send.at[lax.rem(step, CASC)], ws_send.at[lax.rem(step, CASC)])

        return carry

    lax.fori_loop(0, STEPS, drain, jnp.int32(0))


def shards(measured, maps, mask, first_filters, second_filters, step_sizes, cotangent):
    tables = [jnp.asarray(table) for table in constants()]
    dma = pltpu.SemaphoreType.DMA
    field = pltpu.VMEM((2, LINES, LANES), F32)
    scratch = [
        field, field, field,
        pltpu.VMEM((SLICES, LINES), jnp.int32),
        pltpu.VMEM((18, 1, HIDDEN), F32),
        pltpu.VMEM((18, 1, HIDDEN), F32),
    ]
    whole_tables = tables[:5]
    scratch += [pltpu.VMEM(table.shape, table.dtype) for table in whole_tables]
    scratch += [
        pltpu.VMEM((48, LANES), F32),
        pltpu.VMEM((32, LANES), F32),
        dma((13,)),
        pltpu.VMEM((LINES, LANES), F32),
        pltpu.VMEM((3, 2, LINES, LANES), F32),
        pltpu.VMEM((8, LANES, LANES), F32),
        pltpu.VMEM((2, QUARTER, LANES), F32),
        pltpu.VMEM((COILS, QUARTER, LANES), F32),
        pltpu.VMEM((8, SLICES * COILS, LANES), F32),
        pltpu.VMEM((4, 2, SLICES, LANES), F32),
        pltpu.VMEM((8, SLICES, LANES), F32),
        pltpu.VMEM((SLICES * 16, LANES), F32),
        pltpu.VMEM((COILS, 16, LANES), F32),
        pltpu.VMEM((SLICES * 16, LANES), F32),
        pltpu.VMEM((COILS, 16, LANES), F32),
        pltpu.VMEM((CASC, 24, LANES), F32),
        pltpu.VMEM((256, 256), BF16),
        pltpu.VMEM((64, 768), BF16),
        pltpu.VMEM((STEPS, 5, 8, LANES), F32),
        pltpu.VMEM((STEPS, SLICES, 8, LANES), F32),
        pltpu.VMEM((CASC, 256, 3 * LANES), F32),
        pltpu.VMEM((CASC, 256, LANES), F32),
        pltpu.VMEM((CASC + 1, 72, LANES), F32),
        pltpu.VMEM((256, 3 * LANES), F32),
        pltpu.VMEM((4, 256, 768), BF16),
        pltpu.VMEM((8, LANES), F32),
        pltpu.VMEM((8, LANES), F32),
        pltpu.VMEM((8, LANES), F32),
        pltpu.VMEM((CASC, 8, LANES), F32),
        pltpu.VMEM((SLICES * 8, LANES), F32),
        pltpu.VMEM((SLICES * 8, LANES), F32),
        pltpu.VMEM((CASC, 2, QUARTER, LANES), F32),
        pltpu.VMEM((4, 2, QUARTER, LANES), F32),
        pltpu.VMEM((2, 4, 2, SLICES * 8, LANES), F32),
        pltpu.VMEM((4, 8, LANES), F32),
        pltpu.VMEM((2, SLICES, 4, 8, LANES), F32),
        pltpu.VMEM((CASC, 24, LANES), F32),
        pltpu.VMEM((WIDTH, 24, LANES), F32),
        pltpu.VMEM((2, 24, LANES), F32),
        pltpu.VMEM((8, 24, LANES), F32),
        dma, dma, dma, dma, dma, dma, dma, dma,
        dma((STEPS,)), dma((STEPS,)), dma((STEPS,)), dma((STEPS,)), dma((STEPS,)),
        dma, dma, dma, dma, dma, dma, dma((2,)), dma((2,)),
        dma((CASC,)), dma, dma, dma, dma, dma,
    ]
    there = pl.BlockSpec(memory_space=pltpu.HBM)
    whole = pl.BlockSpec(memory_space=pltpu.VMEM)
    first = jnp.transpose(first_filters, (2, 0, 1))
    second = jnp.transpose(second_filters, (1, 0, 2))
    operands = [measured[0], maps[0], cotangent[0], mask, first, second]
    grad_k, grad_w = pl.pallas_call(
        kernel,
        out_shape=[
            jax.ShapeDtypeStruct((2, LINES, LANES), F32),
            jax.ShapeDtypeStruct((19, 1, LANES), F32),
        ],
        in_specs=[there] * 6 + [pl.BlockSpec(memory_space=pltpu.SMEM)] + [there] * len(tables),
        out_specs=[whole, whole],
        scratch_shapes=scratch,
        compiler_params=pltpu.CompilerParams(
            collective_id=0, has_side_effects=True, vmem_limit_bytes=58 * 1024 * 1024
        ),
        name="cascades",
    )(*operands, step_sizes, *tables)
    first = jnp.transpose(grad_w[:18, :, :64], (1, 2, 0))
    second = jnp.transpose(grad_w[:18, :, 64:], (1, 0, 2))
    return grad_k[None, None], first, second, grad_w[18, 0, :1]


def solution(mesh):
    in_specs = (
        P("coil", None, None, None),
        P("coil", None, None, None),
        P(),
        P("segment", None, None),
        P("segment", None, None),
        P("segment"),
        P("coil", None, None, None),
    )
    out_specs = (
        P("segment", "coil", None, None, None),
        P("segment", None, None),
        P("segment", None, None),
        P("segment"),
    )
    return jax.shard_map(shards, mesh=mesh, in_specs=in_specs, out_specs=out_specs, check_vma=False)
```
